32 devices in a mesh: inner: 4 (over y, x), outer: 8 (over z, core).
Axes of the slice: x: 2, y: 2, z: 4, core: 2. Of those that a mesh axis runs over, the one named last changes fastest.
Arguments:
- queries: bfloat16 [4096, 512], P(('inner', 'outer')), may hold values from -6 to 6
- keys_values: bfloat16 [4096, 256], P(('inner', 'outer')), may hold values from -6 to 6
- outputs: bfloat16 [4096, 512], P(('inner', 'outer')), may hold values from -3 to 3
- d_out: bfloat16 [4096, 512], P(('inner', 'outer')), may hold values from -6 to 6
- lse: float32 [4096, 4], P(('inner', 'outer'))
- doc_start: int32 [4096], P(('inner', 'outer')), may hold values from 0 to 4095, as said below
Outputs:
- d_queries: bfloat16 [4096, 512], P(('inner', 'outer'))
- d_keys_values: bfloat16 [4096, 256], P(('inner', 'outer'))
The draws below stay inside these ranges and needn't reach their ends.
Inputs may be any that keep to these rules, and one draw needn't show every extreme that they name: doc_start of a token is the first sequence position of the document that holds it; documents are 8 or fewer runs of consecutive positions, the first starting at position 0.
All inputs are finite; a program needn't handle non-finite values.
Results may differ from the reference program's by a relative error of at most 0.0047.
Values may be sent and summed in bfloat16 or wider, within the bound.
No kernel may reach another device: no remote copies, remote signals or barrier semaphores. Data moves between devices by JAX's collectives and lax.ppermute only.
A program may use at most 64 MiB of HBM per device.

```python
import jax
import jax.numpy as jnp
from jax import lax

HEADS = 4
HD = 128
TOK_DEV = 128
DOCS = 8
GROUP = 4
LOOP = 8
TOKENS = 4096


def sequence_positions_drawn():
    row_ids = jnp.arange(TOKENS, dtype=jnp.int32)
    shard = row_ids // TOK_DEV
    offset = row_ids % TOK_DEV
    half_rows = TOK_DEV // 2
    member = shard // LOOP
    place = shard % LOOP
    band = jnp.where(offset < half_rows, place, 2 * LOOP - 1 - place)
    return band * (GROUP * half_rows) + member * half_rows + offset % half_rows


def document_starts(key):
    cuts = jnp.sort(jax.random.randint(jax.random.fold_in(key, 11), (DOCS - 1,), 1, TOKENS, dtype=jnp.int32))
    sequence = jnp.arange(TOKENS, dtype=jnp.int32)
    seq_start = jnp.max(jnp.where(cuts[None, :] <= sequence[:, None], cuts[None, :], 0), axis=1)
    return seq_start[sequence_positions_drawn()].astype(jnp.int32)


def draw_doc_start(key, part):
    return document_starts(key)


def draw_lse(key, part):
    starts = document_starts(key)
    visible = (sequence_positions_drawn() - starts + 1).astype(jnp.float32)
    offset_key = jax.random.fold_in(key, 23)
    offset = jax.random.uniform(offset_key, (TOKENS, HEADS), jnp.float32, 0.3, 0.8)
    return jnp.log(visible)[:, None] + offset


def level_of(key, dims, shards, least, high):
    gain = 1.0
    for axis_at, parts in shards:
        heights = jax.random.uniform(jax.random.fold_in(jax.random.fold_in(key, 6), axis_at), (parts,), jnp.float32, least / len(shards), high / len(shards))
        gain = gain * jnp.repeat(jnp.exp(heights), dims[axis_at] // parts).reshape((-1,) + (1,) * (len(dims) - 1 - axis_at))
    return gain


def bell_draw(stream_key, dims, width, bound, cuts=(), kind=jnp.bfloat16):
    values = jax.random.normal(stream_key, dims, jnp.float32) * width
    if len(cuts) > 0:
        values = level_of(stream_key, dims, cuts, -0.22, 0.18) * values
    return jnp.clip(values, min=-bound, max=bound).astype(kind)


def setup_inputs(seed: int = 0) -> dict:
    splits = jax.random.split(jax.random.key(seed), 7)
    return {
        "queries": bell_draw(splits[0], (TOKENS, HEADS * HD), 1.0, 6.0, ((0, 32),)),
        "keys_values": bell_draw(splits[1], (TOKENS, 2 * HD), 1.0, 6.0, ((0, 32),)),
        "outputs": bell_draw(splits[2], (TOKENS, HEADS * HD), 0.5, 3.0, ((0, 32),)),
        "d_out": bell_draw(splits[3], (TOKENS, HEADS * HD), 1.0, 6.0, ((0, 32),)),
        "lse": draw_lse(jax.random.fold_in(splits[6], 71), 0),
        "doc_start": draw_doc_start(jax.random.fold_in(splits[6], 71), 0),
    }


def sequence_positions():
    row_ids = jnp.arange(TOKENS, dtype=jnp.int32)
    shard = row_ids // TOK_DEV
    offset = row_ids % TOK_DEV
    half_rows = TOK_DEV // 2
    member = shard // LOOP
    place = shard % LOOP
    band = jnp.where(offset < half_rows, place, 2 * LOOP - 1 - place)
    return band * (GROUP * half_rows) + member * half_rows + offset % half_rows


def rounded(value):
    return lax.optimization_barrier(value.astype(jnp.bfloat16)).astype(value.dtype)


def reference(queries, keys_values, outputs, d_out, lse, doc_start):
    highest = lax.Precision.HIGHEST
    positions = sequence_positions()

    def ordered(value):
        return jnp.zeros_like(value).at[positions].set(value)

    query_heads = ordered(queries).astype(jnp.float32).reshape(TOKENS, HEADS, HD)
    pairs = ordered(keys_values).astype(jnp.float32)
    key_rows = pairs[:, :HD]
    value_rows = pairs[:, HD:]
    grad_heads = ordered(d_out).astype(jnp.float32).reshape(TOKENS, HEADS, HD)
    out_heads = ordered(outputs).astype(jnp.float32).reshape(TOKENS, HEADS, HD)
    log_totals = ordered(lse).astype(jnp.float32)
    starts = ordered(doc_start)
    delta = jnp.sum(grad_heads * out_heads, axis=2)
    score_scale = HD ** -0.5
    block_len = min(512, TOKENS)
    block_count = TOKENS // block_len

    def query_block(accumulator, block_index):
        first = block_index * block_len
        query_part = lax.dynamic_slice_in_dim(query_heads, first, block_len, 0)
        grad_part = lax.dynamic_slice_in_dim(grad_heads, first, block_len, 0)
        log_part = lax.dynamic_slice_in_dim(log_totals, first, block_len, 0).T
        delta_part = lax.dynamic_slice_in_dim(delta, first, block_len, 0).T
        start_part = lax.dynamic_slice_in_dim(starts, first, block_len, 0)
        query_pos = first + jnp.arange(block_len, dtype=jnp.int32)

        def key_block(carry, key_index):
            live = jnp.logical_and(key_index <= block_index, (key_index + 1) * block_len > start_part[0])

            def work(state):
                query_grad, totals = state
                key_first = key_index * block_len
                key_part = lax.dynamic_slice_in_dim(key_rows, key_first, block_len, 0)
                value_part = lax.dynamic_slice_in_dim(value_rows, key_first, block_len, 0)
                key_pos = key_first + jnp.arange(block_len, dtype=jnp.int32)
                mask = jnp.logical_and(key_pos[None, :] <= query_pos[:, None], key_pos[None, :] >= start_part[:, None])
                score = jnp.einsum("qhd,kd->hqk", query_part, key_part, precision=highest) * score_scale
                prob = jnp.where(mask[None], jnp.exp(score - log_part[:, :, None]), 0.0)
                dprob = jnp.einsum("qhd,kd->hqk", grad_part, value_part, precision=highest)
                dscore = rounded(prob * (dprob - delta_part[:, :, None]))
                prob_half = rounded(prob)
                query_grad = query_grad + jnp.einsum("hqk,kd->qhd", dscore, key_part, precision=highest) * score_scale
                key_grad = jnp.einsum("hqk,qhd->kd", dscore, query_part, precision=highest) * score_scale
                value_grad = jnp.einsum("hqk,qhd->kd", prob_half, grad_part, precision=highest)
                piece = lax.dynamic_slice_in_dim(totals, key_first, block_len, 0)
                piece = piece + jnp.concatenate([key_grad, value_grad], axis=1)
                totals = lax.dynamic_update_slice_in_dim(totals, piece, key_first, 0)
                return query_grad, totals

            def skip(state):
                return state

            return lax.cond(live, work, skip, carry), None

        start_grad = jnp.zeros((block_len, HEADS, HD), jnp.float32)
        (query_grad, accumulator), _ = lax.scan(key_block, (start_grad, accumulator), jnp.arange(block_count, dtype=jnp.int32))
        return accumulator, query_grad

    totals, query_blocks = lax.scan(query_block, jnp.zeros((TOKENS, 2 * HD), jnp.float32), jnp.arange(block_count, dtype=jnp.int32))
    query_grad = query_blocks.reshape(TOKENS, HEADS * HD)
    return query_grad[positions].astype(jnp.bfloat16), totals[positions].astype(jnp.bfloat16)
```

```python
import functools
import math

import jax
import jax.numpy as jnp
from jax import lax
from jax.experimental import pallas as pl
from jax.experimental.pallas import tpu as pltpu
from jax.sharding import Mesh
from jax.sharding import PartitionSpec as P

LOG2E = math.log2(math.e)
STAT_ROWS = 32
VMEM_LIMIT = 48 * 1024 * 1024
BF16 = jnp.bfloat16
F32 = jnp.float32
VMEM = pl.BlockSpec(memory_space=pltpu.VMEM)


def peer(place, step, count):
    if count & (count - 1) == 0:
        return place ^ step
    return (place + count - step) % count


def fetch(value, axis, step):
    count = lax.axis_size(axis)
    return lax.ppermute(value, axis, [(peer(i, step, count), i) for i in range(count)])


def give_back(value, axis, step):
    count = lax.axis_size(axis)
    return lax.ppermute(value, axis, [(i, peer(i, step, count)) for i in range(count)])


def three_parts(value):
    high = value.astype(BF16).astype(F32)
    rest = value - high
    middle = rest.astype(BF16).astype(F32)
    return [high, middle, rest - middle]


def pack_kernel(heads, q_ref, g_ref, o_ref, lse_ref, start_ref, pack_ref):
    tok = q_ref.shape[0]
    width = q_ref.shape[1] // heads
    deltas = []
    for h in range(heads):
        cols = slice(h * width, (h + 1) * width)
        q, g = q_ref[:, cols], g_ref[:, cols]
        pack_ref[h * tok : (h + 1) * tok, :] = q
        pack_ref[(heads + h) * tok : (heads + h + 1) * tok, :] = g
        product = g.astype(F32) * o_ref[:, cols].astype(F32)
        deltas.append(jnp.sum(product.T, axis=0, keepdims=True))
    delta = jnp.concatenate(deltas, axis=0)
    starts = start_ref[...]
    rows = three_parts(lse_ref[...]) + three_parts(delta)
    rows += [(starts >> 8).astype(F32), (starts & 255).astype(F32)]
    used = 6 * heads + 2
    rows.append(jnp.zeros((STAT_ROWS - used, tok), F32))
    pack_ref[2 * heads * tok :, :] = jnp.concatenate(rows, axis=0).astype(BF16)


def pack(queries, d_out, outputs, lse, doc_start, heads):
    tok = queries.shape[0]
    width = queries.shape[1] // heads
    return pl.pallas_call(
        functools.partial(pack_kernel, heads),
        out_shape=jax.ShapeDtypeStruct((2 * heads * tok + STAT_ROWS, width), BF16),
        in_specs=[VMEM] * 5,
        out_specs=VMEM,
        name="pack",
    )(queries, d_out, outputs, lse.T, doc_start.reshape(1, tok))


def part_kernel(steps, first, last, heads, sizes, *refs):
    inner, zed = sizes
    packs, refs = refs[: len(steps)], refs[len(steps) :]
    mine, refs = refs[:zed], refs[zed:]
    others, refs = refs[:zed], refs[zed:]
    if first:
        acc = None
    else:
        acc, refs = refs[:2], refs[2:]
    dq_refs, refs = refs[: len(steps)], refs[len(steps) :]
    totals = refs
    me = lax.axis_index("inner")
    z_me = lax.axis_index("z")
    core = lax.axis_index("core")
    tok, width = mine[0].shape[0], mine[0].shape[1] // 2
    half = tok // 2
    band_len = inner * half
    outer = 2 * z_me + core
    scale = width**-0.5
    lane = lax.broadcasted_iota(jnp.int32, (1, tok), 1)
    row = lax.broadcasted_iota(jnp.int32, (tok, 1), 0)

    def position(index, source, member):
        band = jnp.where(index < half, source, 4 * zed - 1 - source)
        return band * band_len + member * half + index % half

    q_info = []
    for step, pack_ref in zip(steps, packs):
        stats = pack_ref[2 * heads * tok :, :].astype(F32)
        lse = stats[:heads] + stats[heads : 2 * heads] + stats[2 * heads : 3 * heads]
        delta = stats[3 * heads : 4 * heads] + stats[4 * heads : 5 * heads] + stats[5 * heads : 6 * heads]
        starts = stats[6 * heads : 6 * heads + 1] * 256.0 + stats[6 * heads + 1 : 6 * heads + 2]
        q_pos = position(lane, outer, peer(me, step, inner))
        q_info.append((lse * LOG2E, delta, starts.astype(jnp.int32), q_pos))

    dq_t = [None] * len(steps)
    chunk = 4 if zed % 4 == 0 else 1
    for side, blocks in enumerate((mine, others)):
        for c0 in range(0, zed, chunk):
            group = blocks[c0 : c0 + chunk]
            keys = jnp.concatenate([b[:, :width] for b in group], axis=0)
            values = jnp.concatenate([b[:, width:] for b in group], axis=0)
            keys_t = keys.T
            k_pos = jnp.concatenate(
                [
                    position(row, 2 * peer(z_me, c0 + j, zed) + (core if side == 0 else 1 - core), me)
                    for j in range(chunk)
                ],
                axis=0,
            )
            dk_sum, dv_sum = None, None
            for n, pack_ref in enumerate(packs):
                lse, delta, starts, q_pos = q_info[n]
                mask = jnp.logical_and(k_pos <= q_pos, k_pos >= starts)
                probs, dscores = [], []
                for h in range(heads):
                    q = pack_ref[h * tok : (h + 1) * tok, :]
                    g = pack_ref[(heads + h) * tok : (heads + h + 1) * tok, :]
                    nt = (((1,), (1,)), ((), ()))
                    s = lax.dot_general(keys, q, nt, preferred_element_type=F32)
                    dp = lax.dot_general(values, g, nt, preferred_element_type=F32)
                    p = jnp.where(mask, jnp.exp2(s * (scale * LOG2E) - lse[h : h + 1]), 0.0)
                    ds = p * (dp - delta[h : h + 1])
                    probs.append(p.astype(BF16))
                    dscores.append(ds.astype(BF16))
                prob = jnp.concatenate(probs, axis=1)
                dscore = jnp.concatenate(dscores, axis=1)
                dv = jnp.dot(prob, pack_ref[heads * tok : 2 * heads * tok, :], preferred_element_type=F32)
                dk = jnp.dot(dscore, pack_ref[: heads * tok, :], preferred_element_type=F32)
                dq = jnp.dot(keys_t, dscore, preferred_element_type=F32)
                dq_t[n] = dq if dq_t[n] is None else dq_t[n] + dq
                dk_sum = dk if dk_sum is None else dk_sum + dk
                dv_sum = dv if dv_sum is None else dv_sum + dv
            here = slice(c0 * tok, (c0 + chunk) * tok)
            dk_sum = dk_sum * scale
            if not first:
                dk_sum = dk_sum + acc[side][here, :width]
                dv_sum = dv_sum + acc[side][here, width:]
            totals[side][here, :width] = dk_sum.astype(totals[side].dtype)
            totals[side][here, width:] = dv_sum.astype(totals[side].dtype)
    for n, dq_ref in enumerate(dq_refs):
        for h in range(heads):
            block = dq_t[n][:, h * tok : (h + 1) * tok] * scale
            dq_ref[:, h * width : (h + 1) * width] = block.T.astype(dq_ref.dtype)


def part(steps, packs, mine, others, acc, last, heads, sizes):
    tok, two = mine[0].shape
    width = two // 2
    zed = sizes[1]
    dq_types = [F32 if s == 0 else BF16 for s in steps]
    outs = [jax.ShapeDtypeStruct((tok, heads * width), t) for t in dq_types]
    outs += [jax.ShapeDtypeStruct((zed * tok, two), F32), jax.ShapeDtypeStruct((zed * tok, two), BF16 if last else F32)]
    args = list(packs) + list(mine) + list(others) + list(acc or [])
    elements = len(steps) * heads * tok * 2 * zed * tok
    result = pl.pallas_call(
        functools.partial(part_kernel, steps, acc is None, last, heads, sizes),
        out_shape=outs,
        in_specs=[VMEM] * len(args),
        out_specs=[VMEM] * len(outs),
        compiler_params=pltpu.CompilerParams(vmem_limit_bytes=VMEM_LIMIT),
        cost_estimate=pl.CostEstimate(flops=elements * width * 10, bytes_accessed=1 << 20, transcendentals=elements),
        name="part",
    )(*args)
    return result[: len(steps)], result[len(steps) :]


def join_kernel(kept_ref, other_ref, *outs):
    tok = outs[0].shape[0]
    for s, out in enumerate(outs):
        here = slice(s * tok, (s + 1) * tok)
        out[...] = (kept_ref[here, :] + other_ref[here, :].astype(F32)).astype(out.dtype)


def join(kept, other, zed):
    tok, two = kept.shape[0] // zed, kept.shape[1]
    outs = [jax.ShapeDtypeStruct((tok, two), F32 if s == 0 else BF16) for s in range(zed)]
    return pl.pallas_call(
        join_kernel, out_shape=outs, in_specs=[VMEM] * 2, out_specs=[VMEM] * zed, name="join"
    )(kept, other)


def total_kernel(*refs):
    out = refs[-1]
    total = refs[0][...]
    for ref in refs[1:-1]:
        total = total + ref[...].astype(F32)
    out[...] = total.astype(out.dtype)


def total(values):
    return pl.pallas_call(
        total_kernel,
        out_shape=jax.ShapeDtypeStruct(values[0].shape, BF16),
        in_specs=[VMEM] * len(values),
        out_specs=VMEM,
        name="total",
    )(*values)


def on_device(queries, keys_values, outputs, d_out, lse, doc_start):
    inner = lax.axis_size("inner")
    zed = lax.axis_size("z")
    heads = lse.shape[1]
    sizes = (inner, zed)
    own = pack(queries, d_out, outputs, lse, doc_start, heads)
    packs = [own] + [fetch(own, "inner", s) for s in range(1, inner)]
    mine = [keys_values] + [fetch(keys_values, "z", s) for s in range(1, zed)]
    others = [fetch(kv, "core", 1) for kv in mine]
    groups = [[s] for s in range(inner)]
    acc = None
    dqs = []
    for steps in groups:
        got, acc = part(steps, [packs[s] for s in steps], mine, others, acc, steps is groups[-1], heads, sizes)
        dqs += got
    dq_home = [dqs[0]] + [give_back(dqs[s], "inner", s) for s in range(1, inner)]
    kept, sent = acc
    joined = join(kept, fetch(sent, "core", 1), zed)
    dkv_home = [joined[0]] + [give_back(joined[s], "z", s) for s in range(1, zed)]
    return (total(dq_home), total(dkv_home))


def solution(mesh):
    inner, outer = mesh.shape["inner"], mesh.shape["outer"]
    split = Mesh(mesh.devices.reshape(inner, outer // 2, 2), ("inner", "z", "core"))
    rows = P(("inner", "z", "core"), None)
    return jax.shard_map(
        on_device,
        mesh=split,
        in_specs=(rows, rows, rows, rows, rows, P(("inner", "z", "core"))),
        out_specs=(rows, rows),
        check_vma=False,
    )
```

```python
import functools
import math

import jax
import jax.numpy as jnp
from jax import lax
from jax.experimental import pallas as pl
from jax.experimental.pallas import tpu as pltpu
from jax.sharding import Mesh
from jax.sharding import PartitionSpec as P

LOG2E = math.log2(math.e)
STATS = 8
VMEM_LIMIT = 32 * 1024 * 1024
SMALL_LIMIT = 8 * 1024 * 1024
BF16 = jnp.bfloat16
F32 = jnp.float32
VMEM = pl.BlockSpec(memory_space=pltpu.VMEM)


def peer(place, step, count):
    if count & (count - 1) == 0:
        return place ^ step
    return (place + count - step) % count


def fetch(value, axis, step):
    count = lax.axis_size(axis)
    return lax.ppermute(value, axis, [(peer(i, step, count), i) for i in range(count)])


def give_back(value, axis, step):
    count = lax.axis_size(axis)
    return lax.ppermute(value, axis, [(i, peer(i, step, count)) for i in range(count)])


def three_parts(value):
    high = value.astype(BF16).astype(F32)
    rest = value - high
    middle = rest.astype(BF16).astype(F32)
    return [high, middle, rest - middle]


def pack_kernel(heads, q_ref, g_ref, o_ref, lse_ref, start_ref, pack_ref):
    tok = q_ref.shape[0]
    width = q_ref.shape[1] // heads
    half = tok // 2
    lanes = heads * half
    rows = []
    lse = lse_ref[...]
    starts = start_ref[...]
    for late in range(2):
        here = slice(late * half, (late + 1) * half)
        products = []
        for h in range(heads):
            cols = slice(h * width, (h + 1) * width)
            q, g = q_ref[here, cols], g_ref[here, cols]
            first = late * lanes + h * half
            pack_ref[first : first + half, :] = q
            pack_ref[2 * lanes + first : 2 * lanes + first + half, :] = g
            products.append(g.astype(F32) * o_ref[here, cols].astype(F32))
        delta = jnp.sum(jnp.concatenate(products, axis=0).T, axis=0, keepdims=True)
        log_part = jnp.concatenate([lse[h : h + 1, here] for h in range(heads)], axis=1)
        start = jnp.concatenate([starts[:, here]] * heads, axis=1)
        stats = three_parts(log_part) + three_parts(delta)
        stats += [(start >> 8).astype(F32), (start & 255).astype(F32)]
        for value in stats:
            rows += [value[:, c : c + width] for c in range(0, lanes, width)]
    pack_ref[4 * lanes :, :] = jnp.concatenate(rows, axis=0).astype(BF16)


def pack(queries, d_out, outputs, lse, doc_start, heads):
    tok = queries.shape[0]
    width = queries.shape[1] // heads
    stat_rows = STATS * heads * tok // width
    return pl.pallas_call(
        functools.partial(pack_kernel, heads),
        out_shape=jax.ShapeDtypeStruct((2 * heads * tok + stat_rows, width), BF16),
        in_specs=[VMEM] * 5,
        out_specs=VMEM,
        compiler_params=pltpu.CompilerParams(vmem_limit_bytes=SMALL_LIMIT),
        name="pack",
    )(queries, d_out, outputs, lse.T, doc_start.reshape(1, tok))


def part_kernel(step, first, last, heads, sizes, *refs):
    inner, zed = sizes
    pack_ref, refs = refs[0], refs[1:]
    if first:
        blocks, refs = refs[: 2 * zed], refs[2 * zed :]
        dq_ref, acc_ref, k_ref, v_ref, kt_ref, dqt_ref = refs
    else:
        k_ref, v_ref, kt_ref, acc_in, dq_ref, acc_ref = refs[:6]
        dqt_ref = refs[-1]
    me = lax.axis_index("inner")
    z_me = lax.axis_index("z")
    core = lax.axis_index("core")
    outer = 2 * z_me + core
    tok, width = dq_ref.shape[0], dq_ref.shape[1] // heads
    half = tok // 2
    lanes = heads * half
    front = zed * tok
    band_len = inner * half
    bands = 4 * zed
    scale = width**-0.5
    nt = (((1,), (1,)), ((), ()))

    def rows_of(step, other):
        source = 2 * peer(z_me, step, zed) + (1 - core if other else core)
        return [pl.ds(pl.multiple_of(late * front + source * half, half), half) for late in range(2)]

    if first:
        for n, block in enumerate(blocks):
            for late, here in enumerate(rows_of(n % zed, n >= zed)):
                k_ref[here, :] = block[late * half : (late + 1) * half, :width]
                v_ref[here, :] = block[late * half : (late + 1) * half, width:]
        kt_ref[...] = k_ref[...].T

    per = lanes // width
    member = peer(me, step, inner)
    lane = lax.broadcasted_iota(jnp.int32, (1, lanes), 1) % half
    row = lax.broadcasted_iota(jnp.int32, (tok, 1), 0)
    rows = pack_ref[4 * lanes :, :].astype(F32)
    info = []
    for late in range(2):

        def stat(n):
            at = (late * STATS + n) * per
            return jnp.concatenate([rows[at + i : at + i + 1] for i in range(per)], axis=1)

        lse = (stat(0) + stat(1) + stat(2)) * LOG2E
        delta = stat(3) + stat(4) + stat(5)
        start = (stat(6) * 256.0 + stat(7)).astype(jnp.int32)
        band = bands - 1 - outer if late else outer
        info.append((lse, delta, start, band * band_len + member * half + lane))

    def pick(early, pair):
        return jnp.where(early, pair[0], pair[1])

    def tile(keys, values, q, g, lse, delta, mask):
        s = lax.dot_general(keys, q, nt, preferred_element_type=F32)
        dp = lax.dot_general(values, g, nt, preferred_element_type=F32)
        prob = jnp.where(mask, jnp.exp2(s * (scale * LOG2E) - lse), 0.0)
        dscore = prob * (dp - delta)
        return prob.astype(BF16), dscore.astype(BF16)

    lse, delta, start, _ = info[1]
    pos = jnp.concatenate(
        [(2 * j + row // half) * band_len + me * half + row % half for j in range(zed)], axis=0
    )
    q_late = pack_ref[lanes : 2 * lanes, :]
    g_late = pack_ref[3 * lanes : 4 * lanes, :]
    prob, dscore = tile(k_ref[:front, :], v_ref[:front, :], q_late, g_late, lse, delta, pos >= start)
    dk = jnp.dot(dscore, q_late, preferred_element_type=F32)
    dv = jnp.dot(prob, g_late, preferred_element_type=F32)
    dqt_ref[:, lanes:] = jnp.dot(kt_ref[:, :front], dscore, preferred_element_type=F32)
    dqt_ref[:, :lanes] = jnp.zeros((width, lanes), F32)
    if first:
        acc_ref[:front, :width] = dk
        acc_ref[:front, width:] = dv
        acc_ref[front:, :] = jnp.zeros((front, 2 * width), F32)
    else:
        acc_ref[:front, :width] = acc_in[:front, :width] + dk
        acc_ref[:front, width:] = acc_in[:front, width:] + dv
        acc_ref[front:, :] = acc_in[front:, :]

    done = []
    for t in range(zed + 1):
        early = t <= z_me
        j = jnp.where(early, t, t - 1)
        first_key = pl.multiple_of(jnp.where(early, 0, front) + j * tok, tok)
        first_query = pl.multiple_of(jnp.where(early, 0, lanes), lanes)
        source = 2 * j + row // half
        band = jnp.where(early, source, bands - 1 - source)
        pos = band * band_len + me * half + row % half
        lse, delta, start, q_pos = (pick(early, (a, b)) for a, b in zip(*info))
        keys = pl.ds(first_key, tok)
        q = pack_ref[pl.ds(first_query, lanes), :]
        g = pack_ref[pl.ds(pl.multiple_of(2 * lanes + first_query, lanes), lanes), :]
        mask = jnp.logical_and(pos <= q_pos, pos >= start)
        prob, dscore = tile(k_ref[keys, :], v_ref[keys, :], q, g, lse, delta, mask)
        done.append((keys, pl.ds(first_query, lanes), q, g, prob, dscore))
    parts = []
    for keys, here, q, g, prob, dscore in done:
        dk = jnp.dot(dscore, q, preferred_element_type=F32)
        dv = jnp.dot(prob, g, preferred_element_type=F32)
        dq = jnp.dot(kt_ref[:, keys], dscore, preferred_element_type=F32)
        parts.append((keys, here, dk, dv, dq))
    for keys, here, dk, dv, dq in parts:
        acc_ref[keys, :width] += dk
        acc_ref[keys, width:] += dv
        dqt_ref[:, here] += dq

    for late in range(2):
        turned = (dqt_ref[:, late * lanes : (late + 1) * lanes] * scale).T.astype(dq_ref.dtype)
        for h in range(heads):
            dq_ref[late * half : (late + 1) * half, h * width : (h + 1) * width] = turned[h * half : (h + 1) * half]

    if last:
        kept_ref, sent_ref = refs[6:8]
        for other, out in enumerate((kept_ref, sent_ref)):
            for s in range(zed):
                for late, here in enumerate(rows_of(s, other)):
                    to = slice(s * tok + late * half, s * tok + (late + 1) * half)
                    out[to, :width] = (acc_ref[here, :width] * scale).astype(out.dtype)
                    out[to, width:] = acc_ref[here, width:].astype(out.dtype)


def part(step, packed, state, last, heads, sizes, tok, width):
    zed = sizes[1]
    first = step == 0
    keys = 2 * zed * tok
    outs = [jax.ShapeDtypeStruct((tok, heads * width), F32 if first else BF16)]
    acc = jax.ShapeDtypeStruct((keys, 2 * width), F32)
    scratch = [pltpu.VMEM((width, heads * tok), F32)]
    if first:
        outs += [acc] + [jax.ShapeDtypeStruct(s, BF16) for s in ((keys, width), (keys, width), (width, keys))]
    else:
        outs += [acc]
    if last:
        outs += [jax.ShapeDtypeStruct((zed * tok, 2 * width), t) for t in (F32, BF16)]
    args = [packed] + list(state)
    elements = heads * tok * keys * 9 // 16
    return pl.pallas_call(
        functools.partial(part_kernel, step, first, last, heads, sizes),
        out_shape=outs,
        in_specs=[VMEM] * len(args),
        out_specs=[VMEM] * len(outs),
        scratch_shapes=scratch,
        compiler_params=pltpu.CompilerParams(vmem_limit_bytes=VMEM_LIMIT),
        cost_estimate=pl.CostEstimate(flops=elements * width * 10, bytes_accessed=1 << 20, transcendentals=elements),
        name="part",
    )(*args)


def join_kernel(kept_ref, other_ref, *outs):
    tok = outs[0].shape[0]
    for s, out in enumerate(outs):
        here = slice(s * tok, (s + 1) * tok)
        out[...] = (kept_ref[here, :] + other_ref[here, :].astype(F32)).astype(out.dtype)


def join(kept, other, zed):
    tok, two = kept.shape[0] // zed, kept.shape[1]
    outs = [jax.ShapeDtypeStruct((tok, two), F32 if s == 0 else BF16) for s in range(zed)]
    return pl.pallas_call(
        join_kernel, out_shape=outs, in_specs=[VMEM] * 2, out_specs=[VMEM] * zed, name="join",
        compiler_params=pltpu.CompilerParams(vmem_limit_bytes=SMALL_LIMIT),
    )(kept, other)


def total_kernel(*refs):
    out = refs[-1]
    total = refs[0][...]
    for ref in refs[1:-1]:
        total = total + ref[...].astype(F32)
    out[...] = total.astype(out.dtype)


def total(values):
    return pl.pallas_call(
        total_kernel,
        out_shape=jax.ShapeDtypeStruct(values[0].shape, BF16),
        in_specs=[VMEM] * len(values),
        out_specs=VMEM,
        compiler_params=pltpu.CompilerParams(vmem_limit_bytes=SMALL_LIMIT),
        name="total",
    )(*values)


def on_device(queries, keys_values, outputs, d_out, lse, doc_start):
    inner = lax.axis_size("inner")
    zed = lax.axis_size("z")
    heads = lse.shape[1]
    sizes = (inner, zed)
    own = pack(queries, d_out, outputs, lse, doc_start, heads)
    packs = [own] + [fetch(own, "inner", s) for s in range(1, inner)]
    mine = [keys_values] + [fetch(keys_values, "z", s) for s in range(1, zed)]
    others = [fetch(kv, "core", 1) for kv in mine]
    tok, width = keys_values.shape[0], keys_values.shape[1] // 2
    dqs = []
    state = mine + others
    for s in range(inner):
        out = part(s, packs[s], state, s == inner - 1, heads, sizes, tok, width)
        dqs.append(out[0])
        state = (list(out[2:5]) if s == 0 else state[:3]) + [out[1]]
    kept, sent = out[2:4]
    dq_home = [dqs[0]] + [give_back(dqs[s], "inner", s) for s in range(1, inner)]
    joined = join(kept, fetch(sent, "core", 1), zed)
    dkv_home = [joined[0]] + [give_back(joined[s], "z", s) for s in range(1, zed)]
    return (total(dq_home), total(dkv_home))


def solution(mesh):
    inner, outer = mesh.shape["inner"], mesh.shape["outer"]
    split = Mesh(mesh.devices.reshape(inner, outer // 2, 2), ("inner", "z", "core"))
    rows = P(("inner", "z", "core"), None)
    return jax.shard_map(
        on_device,
        mesh=split,
        in_specs=(rows, rows, rows, rows, rows, P(("inner", "z", "core"))),
        out_specs=(rows, rows),
        check_vma=False,
    )
```

```python
import functools
import math

import jax
import jax.numpy as jnp
from jax import lax
from jax.experimental import pallas as pl
from jax.experimental.pallas import tpu as pltpu
from jax.sharding import Mesh
from jax.sharding import PartitionSpec as P

LOG2E = math.log2(math.e)
STATS = 8
PIECES = 4
PART_COST = 200000000
VMEM_LIMIT = 32 * 1024 * 1024
SMALL_LIMIT = 8 * 1024 * 1024
BF16 = jnp.bfloat16
F32 = jnp.float32
VMEM = pl.BlockSpec(memory_space=pltpu.VMEM)


def power_of_two(count):
    return count & (count - 1) == 0


def peer(place, step, count):
    if power_of_two(count):
        return place ^ step
    return (place + count - step) % count


def query_rounds(inner):
    steps = list(range(1, inner))
    return [tuple(steps[n : n + 2]) for n in range(0, inner - 1, 2)]


def inner_pairs(steps, count):
    return [(2 * peer(i, steps[min(c, len(steps) - 1)], count) + c, 2 * i + c) for i in range(count) for c in range(2)]


def fetch(value, steps):
    return lax.ppermute(value, ("inner", "core"), inner_pairs(steps, lax.axis_size("inner")))


def give_back(value, steps):
    pairs = inner_pairs(steps, lax.axis_size("inner"))
    return lax.ppermute(value, ("inner", "core"), [(b, a) for a, b in pairs])


def fetch_z(value, step):
    count = lax.axis_size("z")
    return lax.ppermute(value, "z", [(peer(z, step, count), z) for z in range(count)])


def give_back_z(value, step):
    count = lax.axis_size("z")
    return lax.ppermute(value, "z", [(z, peer(z, step, count)) for z in range(count)])


def swap_cores(value):
    return lax.ppermute(value, "core", [(0, 1), (1, 0)])


def three_parts(value):
    high = value.astype(BF16).astype(F32)
    rest = value - high
    middle = rest.astype(BF16).astype(F32)
    return [high, middle, rest - middle]


def pack_kernel(heads, *refs):
    sources, pack_ref, places, arrived = refs[:5], refs[5], refs[6:11], refs[11]
    copies = [pltpu.make_async_copy(a, b, arrived.at[i]) for i, (a, b) in enumerate(zip(sources, places))]
    for copy in copies:
        copy.start()
    for copy in copies:
        copy.wait()
    q_ref, g_ref, o_ref, lse_ref, start_ref = places
    tok = q_ref.shape[0]
    width = q_ref.shape[1] // heads
    half = tok // 2
    lanes = heads * half
    rows = []
    lse = lse_ref[...]
    starts = start_ref[...]
    for late in range(2):
        here = slice(late * half, (late + 1) * half)
        products = []
        for h in range(heads):
            cols = slice(h * width, (h + 1) * width)
            q, g = q_ref[here, cols], g_ref[here, cols]
            first = late * lanes + h * half
            pack_ref[first : first + half, :] = q
            pack_ref[2 * lanes + first : 2 * lanes + first + half, :] = g
            products.append(g.astype(F32) * o_ref[here, cols].astype(F32))
        delta = jnp.sum(jnp.concatenate(products, axis=0).T, axis=0, keepdims=True)
        log_part = jnp.concatenate([lse[h : h + 1, here] for h in range(heads)], axis=1)
        start = jnp.concatenate([starts[:, here]] * heads, axis=1)
        stats = three_parts(log_part) + three_parts(delta)
        stats += [(start >> 8).astype(F32), (start & 255).astype(F32)]
        for value in stats:
            rows += [value[:, c : c + width] for c in range(0, lanes, width)]
    pack_ref[4 * lanes :, :] = jnp.concatenate(rows, axis=0).astype(BF16)


def pack(queries, d_out, outputs, lse, doc_start, heads):
    tok = queries.shape[0]
    width = queries.shape[1] // heads
    stat_rows = STATS * heads * tok // width
    args = (queries, d_out, outputs, lse.T, doc_start.reshape(1, tok))
    args = [pltpu.with_memory_space_constraint(a, pltpu.HBM) for a in args]
    return pl.pallas_call(
        functools.partial(pack_kernel, heads),
        out_shape=jax.ShapeDtypeStruct((2 * heads * tok + stat_rows, width), BF16),
        in_specs=[pl.BlockSpec(memory_space=pltpu.HBM)] * 5,
        out_specs=VMEM,
        scratch_shapes=[pltpu.VMEM(a.shape, a.dtype) for a in args] + [pltpu.SemaphoreType.DMA((5,))],
        compiler_params=pltpu.CompilerParams(vmem_limit_bytes=SMALL_LIMIT),
        name="pack",
    )(*args)


def stack_kernel(*refs):
    out = refs[-1]
    rows = refs[0].shape[0]
    for n, ref in enumerate(refs[:-1]):
        out[n * rows : (n + 1) * rows, :] = ref[...]


def stack(*values):
    rows, columns = values[0].shape
    return pl.pallas_call(
        stack_kernel,
        out_shape=jax.ShapeDtypeStruct((len(values) * rows, columns), values[0].dtype),
        in_specs=[VMEM] * len(values),
        out_specs=VMEM,
        compiler_params=pltpu.CompilerParams(vmem_limit_bytes=SMALL_LIMIT),
        name="stack",
    )(*values)


def part_kernel(steps, first, last, heads, sizes, *refs):
    inner, zed = sizes
    pack_ref, refs = refs[0], refs[1:]
    if first:
        blocks, refs = refs[:4], refs[4:]
        dq_ref, acc_ref, k_ref, v_ref, kt_ref, dqt_ref = refs
    elif last:
        k_ref, v_ref, kt_ref, acc_in, dq_ref, kept_ref, sent_ref, dqt_ref, acc_ref = refs
    else:
        k_ref, v_ref, kt_ref, acc_in, dq_ref, acc_ref, dqt_ref = refs
    me = lax.axis_index("inner")
    z_me = lax.axis_index("z")
    core = lax.axis_index("core")
    width = dq_ref.shape[1] // heads
    tok = k_ref.shape[0] // (2 * zed)
    half = tok // 2
    lanes = heads * half
    front = zed * tok
    band_len = inner * half
    bands = 4 * zed
    scale = width**-0.5
    nt = (((1,), (1,)), ((), ()))
    per = lanes // width
    rows_each = 4 * lanes + STATS * 2 * per
    jobs = pack_ref.shape[0] // rows_each
    lane = lax.broadcasted_iota(jnp.int32, (1, lanes), 1) % half
    row = lax.broadcasted_iota(jnp.int32, (tok, 1), 0)

    if first:
        for n, block in enumerate(blocks):
            steps_here = [0] if n < 2 else range(zed - 1, 0, -1)
            for m, s in enumerate(steps_here):
                source = 2 * peer(z_me, s, zed) + (1 - core if n % 2 else core)
                for late in range(2):
                    here = pl.ds(pl.multiple_of(late * front + source * half, half), half)
                    rows = slice(m * tok + late * half, m * tok + (late + 1) * half)
                    k_ref[here, :] = block[rows, :width]
                    v_ref[here, :] = block[rows, width:]
        kt_ref[...] = k_ref[...].T

    member = peer(me, jnp.where(core == 0, steps[0], steps[-1]), inner) if steps else me

    def tile(keys, values, q, g, lse, delta, mask):
        s = lax.dot_general(keys, q, nt, preferred_element_type=F32)
        dp = lax.dot_general(values, g, nt, preferred_element_type=F32)
        prob = jnp.where(mask, jnp.exp2(s * (scale * LOG2E) - lse), 0.0)
        dscore = prob * (dp - delta)
        return prob.astype(BF16), dscore.astype(BF16)

    def pick(early, pair):
        return jnp.where(early, pair[0], pair[1])

    for job in range(jobs):
        base = job * rows_each
        outer = 2 * z_me + (core if job == 0 else 1 - core)
        rows = pack_ref[base + 4 * lanes : base + rows_each, :].astype(F32)
        info = []
        for late in range(2):

            def stat(n):
                at = (late * STATS + n) * per
                return jnp.concatenate([rows[at + i : at + i + 1] for i in range(per)], axis=1)

            lse = (stat(0) + stat(1) + stat(2)) * LOG2E
            delta = stat(3) + stat(4) + stat(5)
            start = (stat(6) * 256.0 + stat(7)).astype(jnp.int32)
            band = bands - 1 - outer if late else outer
            info.append((lse, delta, start, band * band_len + member * half + lane))

        lse, delta, start, _ = info[1]
        pos = jnp.concatenate(
            [(2 * j + row // half) * band_len + me * half + row % half for j in range(zed)], axis=0
        )
        q_late = pack_ref[base + lanes : base + 2 * lanes, :]
        g_late = pack_ref[base + 3 * lanes : base + 4 * lanes, :]
        prob, dscore = tile(k_ref[:front, :], v_ref[:front, :], q_late, g_late, lse, delta, pos >= start)
        dk = jnp.dot(dscore, q_late, preferred_element_type=F32)
        dv = jnp.dot(prob, g_late, preferred_element_type=F32)
        dqt_ref[:, lanes:] = jnp.dot(kt_ref[:, :front], dscore, preferred_element_type=F32)
        dqt_ref[:, :lanes] = jnp.zeros((width, lanes), F32)
        if first:
            acc_ref[:front, :width] = dk
            acc_ref[:front, width:] = dv
            acc_ref[front:, :] = jnp.zeros((front, 2 * width), F32)
        else:
            before = acc_in if job == 0 else acc_ref
            acc_ref[:front, :width] = before[:front, :width] + dk
            acc_ref[:front, width:] = before[:front, width:] + dv
            if job == 0:
                acc_ref[front:, :] = acc_in[front:, :]

        done = []
        for t in range(zed + 1):
            early = t <= z_me
            j = jnp.where(early, t, t - 1)
            first_key = pl.multiple_of(jnp.where(early, 0, front) + j * tok, tok)
            first_query = pl.multiple_of(jnp.where(early, 0, lanes), lanes)
            source = 2 * j + row // half
            band = jnp.where(early, source, bands - 1 - source)
            pos = band * band_len + me * half + row % half
            lse, delta, start, q_pos = (pick(early, (a, b)) for a, b in zip(*info))
            keys = pl.ds(first_key, tok)
            q = pack_ref[pl.ds(pl.multiple_of(base + first_query, 16), lanes), :]
            g = pack_ref[pl.ds(pl.multiple_of(base + 2 * lanes + first_query, 16), lanes), :]
            mask = jnp.logical_and(pos <= q_pos, pos >= start)
            prob, dscore = tile(k_ref[keys, :], v_ref[keys, :], q, g, lse, delta, mask)
            done.append((keys, pl.ds(first_query, lanes), q, g, prob, dscore))
        parts = []
        for keys, here, q, g, prob, dscore in done:
            dk = jnp.dot(dscore, q, preferred_element_type=F32)
            dv = jnp.dot(prob, g, preferred_element_type=F32)
            dq = jnp.dot(kt_ref[:, keys], dscore, preferred_element_type=F32)
            parts.append((keys, here, dk, dv, dq))
        for keys, here, dk, dv, dq in parts:
            acc_ref[keys, :width] += dk
            acc_ref[keys, width:] += dv
            dqt_ref[:, here] += dq

        for late in range(2):
            turned = (dqt_ref[:, late * lanes : (late + 1) * lanes] * scale).T.astype(dq_ref.dtype)
            to = slice(job * tok + late * half, job * tok + (late + 1) * half)
            for h in range(heads):
                dq_ref[to, h * width : (h + 1) * width] = turned[h * half : (h + 1) * half]

    if last:
        low = core == 0
        for n in range(2 * zed):
            to = slice(n * half, (n + 1) * half)
            for columns, factor in ((slice(0, width), scale), (slice(width, 2 * width), 1.0)):
                one = acc_ref[n * tok : n * tok + half, columns] * factor
                two = acc_ref[n * tok + half : (n + 1) * tok, columns] * factor
                kept_ref[to, columns] = jnp.where(low, one, two)
                sent_ref[to, columns] = jnp.where(low, two, one).astype(sent_ref.dtype)


def part(steps, packed, state, last, heads, sizes, tok, width):
    zed = sizes[1]
    first = not steps
    jobs = max(1, len(steps))
    keys = 2 * zed * tok
    outs = [jax.ShapeDtypeStruct((jobs * tok, heads * width), F32 if first else BF16)]
    acc = ((keys, 2 * width), F32)
    scratch = [pltpu.VMEM((width, heads * tok), F32)]
    if last:
        outs += [jax.ShapeDtypeStruct((zed * tok, 2 * width), t) for t in (F32, BF16)]
        scratch.append(pltpu.VMEM(*acc))
    else:
        outs.append(jax.ShapeDtypeStruct(*acc))
    if first:
        outs += [jax.ShapeDtypeStruct(s, BF16) for s in ((keys, width), (keys, width), (width, keys))]
    args = [packed] + list(state)
    return pl.pallas_call(
        functools.partial(part_kernel, steps, first, last, heads, sizes),
        out_shape=outs,
        in_specs=[VMEM] * len(args),
        out_specs=[VMEM] * len(outs),
        scratch_shapes=scratch,
        compiler_params=pltpu.CompilerParams(vmem_limit_bytes=VMEM_LIMIT),
        cost_estimate=pl.CostEstimate(flops=jobs * PART_COST, bytes_accessed=1000, transcendentals=0),
        name="part",
    )(*args)


def join_kernel(zed, kept_ref, other_ref, *outs):
    z_me = lax.axis_index("z")
    tok = outs[0].shape[0]
    half = tok // 2
    for s, out in enumerate(outs):
        for late in range(2):
            here = pl.ds(pl.multiple_of((late * zed + peer(z_me, s, zed)) * half, half), half)
            both = kept_ref[here, :] + other_ref[here, :].astype(F32)
            out[late * half : (late + 1) * half, :] = both.astype(out.dtype)


def join(kept, other, zed):
    tok, two = kept.shape[0] // zed, kept.shape[1]
    outs = [jax.ShapeDtypeStruct((tok, two), F32 if s == 0 else BF16) for s in range(zed)]
    return pl.pallas_call(
        functools.partial(join_kernel, zed), out_shape=outs, in_specs=[VMEM] * 2, out_specs=[VMEM] * zed, name="join",
        compiler_params=pltpu.CompilerParams(vmem_limit_bytes=SMALL_LIMIT),
    )(kept, other)


def split_kernel(ref, *outs):
    rows = outs[0].shape[0]
    first = ref.shape[0] - rows * len(outs)
    for n, out in enumerate(outs):
        out[...] = ref[first + n * rows : first + (n + 1) * rows, :]


def split(value, pieces):
    rows, columns = value.shape
    one = jax.ShapeDtypeStruct((rows // 2 // pieces, columns), value.dtype)
    return pl.pallas_call(
        split_kernel,
        out_shape=[one] * pieces,
        in_specs=[VMEM],
        out_specs=[VMEM] * pieces,
        compiler_params=pltpu.CompilerParams(vmem_limit_bytes=SMALL_LIMIT),
        name="split",
    )(value)


def total_kernel(*refs):
    out = refs[-1]
    rows = out.shape[0]
    whole = [ref for ref in refs[:-1] if ref.shape[0] >= rows]
    pieces = [ref for ref in refs[:-1] if ref.shape[0] < rows]
    step = pieces[0].shape[0] if pieces else rows
    for at in range(0, rows, step):
        value = whole[0][at : at + step, :].astype(F32)
        for ref in whole[1:]:
            value = value + ref[at : at + step, :].astype(F32)
        for n, ref in enumerate(pieces):
            if n * step % rows == at:
                value = value + ref[...].astype(F32)
        out[at : at + step, :] = value.astype(out.dtype)


def total(values, rows):
    return pl.pallas_call(
        total_kernel,
        out_shape=jax.ShapeDtypeStruct((rows, values[0].shape[1]), BF16),
        in_specs=[VMEM] * len(values),
        out_specs=VMEM,
        compiler_params=pltpu.CompilerParams(vmem_limit_bytes=SMALL_LIMIT),
        name="total",
    )(*values)


def on_device(queries, keys_values, outputs, d_out, lse, doc_start):
    inner = lax.axis_size("inner")
    zed = lax.axis_size("z")
    heads = lse.shape[1]
    sizes = (inner, zed)
    tok, width = keys_values.shape[0], keys_values.shape[1] // 2
    rounds = query_rounds(inner)
    own = pack(queries, d_out, outputs, lse, doc_start, heads)
    swapped = swap_cores(keys_values)
    own, swapped = lax.optimization_barrier((own, swapped))
    chip = stack(own, swap_cores(own)) if any(len(steps) == 2 for steps in rounds) else None
    packs = [fetch(chip if len(steps) == 2 else own, steps) for steps in rounds]
    mine = [keys_values] + [fetch_z(keys_values, s) for s in range(1, zed)]
    far = list(range(zed - 1, 0, -1))
    arrived = stack(*[mine[s] for s in far])
    out = part((), own, [keys_values, swapped, arrived, swap_cores(arrived)], False, heads, sizes, tok, width)
    dq_parts = [out[0]]
    acc, state = out[1], list(out[2:])
    returned = []
    for steps, packed in zip(rounds, packs):
        last = steps == rounds[-1]
        out = part(steps, packed, state + [acc], last, heads, sizes, tok, width)
        returned.append(give_back(out[0], steps))
        acc = out[1]
    kept, sent = out[1:]
    joined = join(kept, swap_cores(sent), zed)
    dkv_parts = [joined[0]] + [give_back_z(joined[s], s) for s in range(zed - 1, 0, -1)]
    for steps, back in zip(rounds, returned):
        dq_parts.append(back)
        if len(steps) == 2:
            back, dkv_parts[2] = lax.optimization_barrier((back, dkv_parts[2]))
            dq_parts += [swap_cores(piece) for piece in split(back, PIECES)]
    d_queries = total(dq_parts, tok)
    return (d_queries, total(dkv_parts, tok))


def solution(mesh):
    inner, outer = mesh.shape["inner"], mesh.shape["outer"]
    split = Mesh(mesh.devices.reshape(inner, outer // 2, 2), ("inner", "z", "core"))
    rows = P(("inner", "z", "core"), None)
    return jax.shard_map(
        on_device,
        mesh=split,
        in_specs=(rows, rows, rows, rows, rows, P(("inner", "z", "core"))),
        out_specs=(rows, rows),
        check_vma=False,
    )
```

```python
import functools
import math

import jax
import jax.numpy as jnp
from jax import lax
from jax.experimental import pallas as pl
from jax.experimental.pallas import tpu as pltpu
from jax.sharding import Mesh
from jax.sharding import PartitionSpec as P

LOG2E = math.log2(math.e)
STATS = 8
PIECES = 4
PART_COST = 1000
VMEM_LIMIT = 32 * 1024 * 1024
SMALL_LIMIT = 8 * 1024 * 1024
BF16 = jnp.bfloat16
F32 = jnp.float32
VMEM = pl.BlockSpec(memory_space=pltpu.VMEM)


def power_of_two(count):
    return count & (count - 1) == 0


def peer(place, step, count):
    if power_of_two(count):
        return place ^ step
    return (place + count - step) % count


def query_rounds(inner):
    steps = list(range(1, inner))
    return [tuple(steps[n : n + 2]) for n in range(0, inner - 1, 2)]


def inner_pairs(steps, count):
    return [(2 * peer(i, steps[min(c, len(steps) - 1)], count) + c, 2 * i + c) for i in range(count) for c in range(2)]


def fetch(value, steps):
    return lax.ppermute(value, ("inner", "core"), inner_pairs(steps, lax.axis_size("inner")))


def give_back(value, steps):
    pairs = inner_pairs(steps, lax.axis_size("inner"))
    return lax.ppermute(value, ("inner", "core"), [(b, a) for a, b in pairs])


def fetch_z(value, step):
    count = lax.axis_size("z")
    return lax.ppermute(value, "z", [(peer(z, step, count), z) for z in range(count)])


def give_back_z(value, step):
    count = lax.axis_size("z")
    return lax.ppermute(value, "z", [(z, peer(z, step, count)) for z in range(count)])


def swap_cores(value):
    return lax.ppermute(value, "core", [(0, 1), (1, 0)])


def three_parts(value):
    high = value.astype(BF16).astype(F32)
    rest = value - high
    middle = rest.astype(BF16).astype(F32)
    return [high, middle, rest - middle]


def pack_rows(heads, q_ref, g_ref, o_ref, lse_ref, start_ref, pack_ref, base):
    tok = q_ref.shape[0]
    width = q_ref.shape[1] // heads
    half = tok // 2
    lanes = heads * half
    rows = []
    lse = lse_ref[...]
    starts = start_ref[...]
    for late in range(2):
        here = slice(late * half, (late + 1) * half)
        products = []
        for h in range(heads):
            cols = slice(h * width, (h + 1) * width)
            q, g = q_ref[here, cols], g_ref[here, cols]
            first = base + late * lanes + h * half
            pack_ref[first : first + half, :] = q
            pack_ref[2 * lanes + first : 2 * lanes + first + half, :] = g
            products.append(g.astype(F32) * o_ref[here, cols].astype(F32))
        delta = jnp.sum(jnp.concatenate(products, axis=0).T, axis=0, keepdims=True)
        log_part = jnp.concatenate([lse[h : h + 1, here] for h in range(heads)], axis=1)
        start = jnp.concatenate([starts[:, here]] * heads, axis=1)
        stats = three_parts(log_part) + three_parts(delta)
        stats += [(start >> 8).astype(F32), (start & 255).astype(F32)]
        for value in stats:
            rows += [value[:, c : c + width] for c in range(0, lanes, width)]
    first = base + 4 * lanes
    pack_ref[first : first + len(rows), :] = jnp.concatenate(rows, axis=0).astype(BF16)


def pack_kernel(heads, *refs):
    sources, pack_ref, places, arrived = refs[:5], refs[5], refs[6:11], refs[11]
    copies = [pltpu.make_async_copy(a, b, arrived.at[i]) for i, (a, b) in enumerate(zip(sources, places))]
    for copy in copies:
        copy.start()
    for copy in copies:
        copy.wait()
    pack_rows(heads, *places, pack_ref, 0)


def rows_packed(heads, queries):
    tok, columns = queries.shape
    return 2 * heads * tok + STATS * heads * tok // (columns // heads)


def pack(heads, args):
    args = [pltpu.with_memory_space_constraint(a, pltpu.HBM) for a in args]
    return pl.pallas_call(
        functools.partial(pack_kernel, heads),
        out_shape=jax.ShapeDtypeStruct((rows_packed(heads, args[0]), args[0].shape[1] // heads), BF16),
        in_specs=[pl.BlockSpec(memory_space=pltpu.HBM)] * 5,
        out_specs=VMEM,
        scratch_shapes=[pltpu.VMEM(a.shape, a.dtype) for a in args] + [pltpu.SemaphoreType.DMA((5,))],
        compiler_params=pltpu.CompilerParams(vmem_limit_bytes=SMALL_LIMIT),
        name="pack",
    )(*args)


def pack_chip_kernel(heads, *refs):
    own_ref, pack_ref = refs[0], refs[-1]
    rows = own_ref.shape[0]
    pack_ref[:rows, :] = own_ref[...]
    pack_rows(heads, *refs[1:6], pack_ref, rows)


def pack_chip(heads, own, args):
    return pl.pallas_call(
        functools.partial(pack_chip_kernel, heads),
        out_shape=jax.ShapeDtypeStruct((2 * own.shape[0], own.shape[1]), BF16),
        in_specs=[VMEM] * 6,
        out_specs=VMEM,
        compiler_params=pltpu.CompilerParams(vmem_limit_bytes=SMALL_LIMIT),
        name="pack_chip",
    )(own, *args)


def stack_kernel(*refs):
    out = refs[-1]
    rows = refs[0].shape[0]
    for n, ref in enumerate(refs[:-1]):
        out[n * rows : (n + 1) * rows, :] = ref[...]


def stack(*values):
    rows, columns = values[0].shape
    return pl.pallas_call(
        stack_kernel,
        out_shape=jax.ShapeDtypeStruct((len(values) * rows, columns), values[0].dtype),
        in_specs=[VMEM] * len(values),
        out_specs=VMEM,
        compiler_params=pltpu.CompilerParams(vmem_limit_bytes=SMALL_LIMIT),
        name="stack",
    )(*values)


def part_kernel(steps, first, last, heads, sizes, *refs):
    inner, zed = sizes
    pack_ref, refs = refs[0], refs[1:]
    if first:
        blocks, refs = refs[:2], refs[2:]
        dq_ref, acc_ref, k_ref, v_ref, kt_ref, dqt_ref = refs
    elif last:
        k_ref, v_ref, kt_ref, acc_in, dq_ref, kept_ref, sent_ref, dqt_ref, acc_ref = refs
    else:
        k_ref, v_ref, kt_ref, acc_in, dq_ref, acc_ref, dqt_ref = refs
    me = lax.axis_index("inner")
    z_me = lax.axis_index("z")
    core = lax.axis_index("core")
    width = dq_ref.shape[1] // heads
    tok = k_ref.shape[0] // (2 * zed)
    half = tok // 2
    lanes = heads * half
    front = zed * tok
    band_len = inner * half
    bands = 4 * zed
    scale = width**-0.5
    nt = (((1,), (1,)), ((), ()))
    per = lanes // width
    rows_each = 4 * lanes + STATS * 2 * per
    jobs = pack_ref.shape[0] // rows_each
    lane = lax.broadcasted_iota(jnp.int32, (1, lanes), 1) % half
    row = lax.broadcasted_iota(jnp.int32, (tok, 1), 0)

    if first:
        for n, block in enumerate(blocks):
            for m, s in enumerate(range(zed - 1, -1, -1)):
                source = 2 * peer(z_me, s, zed) + (1 - core if n else core)
                for late in range(2):
                    here = pl.ds(pl.multiple_of(late * front + source * half, half), half)
                    rows = slice(m * tok + late * half, m * tok + (late + 1) * half)
                    k_ref[here, :] = block[rows, :width]
                    v_ref[here, :] = block[rows, width:]
        kt_ref[...] = k_ref[...].T

    member = peer(me, jnp.where(core == 0, steps[0], steps[-1]), inner) if steps else me

    def tile(keys, values, q, g, lse, delta, mask):
        s = lax.dot_general(keys, q, nt, preferred_element_type=F32)
        dp = lax.dot_general(values, g, nt, preferred_element_type=F32)
        prob = jnp.where(mask, jnp.exp2(s * (scale * LOG2E) - lse), 0.0)
        dscore = prob * (dp - delta)
        return prob.astype(BF16), dscore.astype(BF16)

    def pick(early, pair):
        return jnp.where(early, pair[0], pair[1])

    for job in range(jobs):
        base = job * rows_each
        outer = 2 * z_me + (core if job == 0 else 1 - core)
        rows = pack_ref[base + 4 * lanes : base + rows_each, :].astype(F32)
        info = []
        for late in range(2):

            def stat(n):
                at = (late * STATS + n) * per
                return jnp.concatenate([rows[at + i : at + i + 1] for i in range(per)], axis=1)

            lse = (stat(0) + stat(1) + stat(2)) * LOG2E
            delta = stat(3) + stat(4) + stat(5)
            start = (stat(6) * 256.0 + stat(7)).astype(jnp.int32)
            band = bands - 1 - outer if late else outer
            info.append((lse, delta, start, band * band_len + member * half + lane))

        lse, delta, start, _ = info[1]
        pos = jnp.concatenate(
            [(2 * j + row // half) * band_len + me * half + row % half for j in range(zed)], axis=0
        )
        q_late = pack_ref[base + lanes : base + 2 * lanes, :]
        g_late = pack_ref[base + 3 * lanes : base + 4 * lanes, :]
        prob, dscore = tile(k_ref[:front, :], v_ref[:front, :], q_late, g_late, lse, delta, pos >= start)
        dk = jnp.dot(dscore, q_late, preferred_element_type=F32)
        dv = jnp.dot(prob, g_late, preferred_element_type=F32)
        dqt_ref[:, lanes:] = jnp.dot(kt_ref[:, :front], dscore, preferred_element_type=F32)
        dqt_ref[:, :lanes] = jnp.zeros((width, lanes), F32)
        if first:
            acc_ref[:front, :width] = dk
            acc_ref[:front, width:] = dv
            acc_ref[front:, :] = jnp.zeros((front, 2 * width), F32)
        else:
            before = acc_in if job == 0 else acc_ref
            acc_ref[:front, :width] = before[:front, :width] + dk
            acc_ref[:front, width:] = before[:front, width:] + dv
            if job == 0:
                acc_ref[front:, :] = acc_in[front:, :]

        done = []
        for t in range(zed + 1):
            early = t <= z_me
            j = jnp.where(early, t, t - 1)
            first_key = pl.multiple_of(jnp.where(early, 0, front) + j * tok, tok)
            first_query = pl.multiple_of(jnp.where(early, 0, lanes), lanes)
            source = 2 * j + row // half
            band = jnp.where(early, source, bands - 1 - source)
            pos = band * band_len + me * half + row % half
            lse, delta, start, q_pos = (pick(early, (a, b)) for a, b in zip(*info))
            keys = pl.ds(first_key, tok)
            q = pack_ref[pl.ds(pl.multiple_of(base + first_query, 16), lanes), :]
            g = pack_ref[pl.ds(pl.multiple_of(base + 2 * lanes + first_query, 16), lanes), :]
            mask = jnp.logical_and(pos <= q_pos, pos >= start)
            prob, dscore = tile(k_ref[keys, :], v_ref[keys, :], q, g, lse, delta, mask)
            done.append((keys, pl.ds(first_query, lanes), q, g, prob, dscore))
        parts = []
        for keys, here, q, g, prob, dscore in done:
            dk = jnp.dot(dscore, q, preferred_element_type=F32)
            dv = jnp.dot(prob, g, preferred_element_type=F32)
            dq = jnp.dot(kt_ref[:, keys], dscore, preferred_element_type=F32)
            parts.append((keys, here, dk, dv, dq))
        for keys, here, dk, dv, dq in parts:
            acc_ref[keys, :width] += dk
            acc_ref[keys, width:] += dv
            dqt_ref[:, here] += dq

        for late in range(2):
            turned = (dqt_ref[:, late * lanes : (late + 1) * lanes] * scale).T.astype(dq_ref.dtype)
            to = slice(job * tok + late * half, job * tok + (late + 1) * half)
            for h in range(heads):
                dq_ref[to, h * width : (h + 1) * width] = turned[h * half : (h + 1) * half]

    if last:
        low = core == 0
        for n in range(2 * zed):
            to = slice(n * half, (n + 1) * half)
            for columns, factor in ((slice(0, width), scale), (slice(width, 2 * width), 1.0)):
                one = acc_ref[n * tok : n * tok + half, columns] * factor
                two = acc_ref[n * tok + half : (n + 1) * tok, columns] * factor
                kept_ref[to, columns] = jnp.where(low, one, two)
                sent_ref[to, columns] = jnp.where(low, two, one).astype(sent_ref.dtype)


def part(steps, packed, state, last, heads, sizes, tok, width):
    zed = sizes[1]
    first = not steps
    jobs = max(1, len(steps))
    keys = 2 * zed * tok
    outs = [jax.ShapeDtypeStruct((jobs * tok, heads * width), F32 if first else BF16)]
    acc = ((keys, 2 * width), F32)
    scratch = [pltpu.VMEM((width, heads * tok), F32)]
    if last:
        outs += [jax.ShapeDtypeStruct((zed * tok, 2 * width), t) for t in (F32, BF16)]
        scratch.append(pltpu.VMEM(*acc))
    else:
        outs.append(jax.ShapeDtypeStruct(*acc))
    if first:
        outs += [jax.ShapeDtypeStruct(s, BF16) for s in ((keys, width), (keys, width), (width, keys))]
    args = [packed] + list(state)
    return pl.pallas_call(
        functools.partial(part_kernel, steps, first, last, heads, sizes),
        out_shape=outs,
        in_specs=[VMEM] * len(args),
        out_specs=[VMEM] * len(outs),
        scratch_shapes=scratch,
        compiler_params=pltpu.CompilerParams(vmem_limit_bytes=VMEM_LIMIT),
        cost_estimate=pl.CostEstimate(flops=jobs * PART_COST, bytes_accessed=1000, transcendentals=0),
        name="part",
    )(*args)


def join_kernel(zed, kept_ref, other_ref, *outs):
    z_me = lax.axis_index("z")
    tok = outs[0].shape[0]
    half = tok // 2
    for s, out in enumerate(outs):
        for late in range(2):
            here = pl.ds(pl.multiple_of((late * zed + peer(z_me, s, zed)) * half, half), half)
            both = kept_ref[here, :] + other_ref[here, :].astype(F32)
            out[late * half : (late + 1) * half, :] = both.astype(out.dtype)


def join(kept, other, zed):
    tok, two = kept.shape[0] // zed, kept.shape[1]
    outs = [jax.ShapeDtypeStruct((tok, two), F32 if s == 0 else BF16) for s in range(zed)]
    return pl.pallas_call(
        functools.partial(join_kernel, zed), out_shape=outs, in_specs=[VMEM] * 2, out_specs=[VMEM] * zed, name="join",
        compiler_params=pltpu.CompilerParams(vmem_limit_bytes=SMALL_LIMIT),
    )(kept, other)


def split_kernel(ref, *outs):
    rows = outs[0].shape[0]
    first = ref.shape[0] - rows * len(outs)
    for n, out in enumerate(outs):
        out[...] = ref[first + n * rows : first + (n + 1) * rows, :]


def split(value, pieces):
    rows, columns = value.shape
    one = jax.ShapeDtypeStruct((rows // 2 // pieces, columns), value.dtype)
    return pl.pallas_call(
        split_kernel,
        out_shape=[one] * pieces,
        in_specs=[VMEM],
        out_specs=[VMEM] * pieces,
        compiler_params=pltpu.CompilerParams(vmem_limit_bytes=SMALL_LIMIT),
        name="split",
    )(value)


def add_up(out, refs):
    rows = out.shape[0]
    whole = [ref for ref in refs if ref.shape[0] >= rows]
    pieces = [ref for ref in refs if ref.shape[0] < rows]
    step = pieces[0].shape[0] if pieces else rows
    for at in range(0, rows, step):
        value = whole[0][at : at + step, :].astype(F32)
        for ref in whole[1:]:
            value = value + ref[at : at + step, :].astype(F32)
        for n, ref in enumerate(pieces):
            if n * step % rows == at:
                value = value + ref[...].astype(F32)
        out[at : at + step, :] = value.astype(out.dtype)


def totals_kernel(counts, *refs):
    first = 0
    for count, out in zip(counts, refs[sum(counts) :]):
        add_up(out, refs[first : first + count])
        first += count


def totals(groups, rows):
    args = [value for values in groups for value in values]
    return pl.pallas_call(
        functools.partial(totals_kernel, [len(values) for values in groups]),
        out_shape=[jax.ShapeDtypeStruct((rows, values[0].shape[1]), BF16) for values in groups],
        in_specs=[VMEM] * len(args),
        out_specs=[VMEM] * len(groups),
        compiler_params=pltpu.CompilerParams(vmem_limit_bytes=SMALL_LIMIT),
        name="totals",
    )(*args)


def on_device(queries, keys_values, outputs, d_out, lse, doc_start):
    inner = lax.axis_size("inner")
    zed = lax.axis_size("z")
    heads = lse.shape[1]
    sizes = (inner, zed)
    tok, width = keys_values.shape[0], keys_values.shape[1] // 2
    rounds = query_rounds(inner)
    inputs = (queries, d_out, outputs, lse.T, doc_start.reshape(1, tok))
    own = pack(heads, inputs)
    chip = None
    if any(len(steps) == 2 for steps in rounds):
        chip = pack_chip(heads, own, [swap_cores(value) for value in inputs])
    packs = [fetch(chip if len(steps) == 2 else own, steps) for steps in rounds]
    mine = [keys_values] + [fetch_z(keys_values, s) for s in range(1, zed)]
    far = list(range(zed - 1, -1, -1))
    arrived = stack(*[mine[s] for s in far])
    out = part((), own, [arrived, swap_cores(arrived)], False, heads, sizes, tok, width)
    dq_parts = [out[0]]
    acc, state = out[1], list(out[2:])
    returned = []
    for steps, packed in zip(rounds, packs):
        last = steps == rounds[-1]
        out = part(steps, packed, state + [acc], last, heads, sizes, tok, width)
        returned.append(give_back(out[0], steps))
        acc = out[1]
    kept, sent = out[1:]
    joined = join(kept, swap_cores(sent), zed)
    dkv_parts = [joined[0]] + [give_back_z(joined[s], s) for s in range(zed - 1, 0, -1)]
    for steps, back in zip(rounds, returned):
        dq_parts.append(back)
        if len(steps) == 2:
            back, dkv_parts[2] = lax.optimization_barrier((back, dkv_parts[2]))
            dq_parts += [swap_cores(piece) for piece in split(back, PIECES)]
    return tuple(totals([dq_parts, dkv_parts], tok))


def solution(mesh):
    inner, outer = mesh.shape["inner"], mesh.shape["outer"]
    split = Mesh(mesh.devices.reshape(inner, outer // 2, 2), ("inner", "z", "core"))
    rows = P(("inner", "z", "core"), None)
    return jax.shard_map(
        on_device,
        mesh=split,
        in_specs=(rows, rows, rows, rows, rows, P(("inner", "z", "core"))),
        out_specs=(rows, rows),
        check_vma=False,
    )
```

```python
import functools
import math

import jax
import jax.numpy as jnp
from jax import lax
from jax.experimental import pallas as pl
from jax.experimental.pallas import tpu as pltpu
from jax.sharding import Mesh
from jax.sharding import PartitionSpec as P

LOG2E = math.log2(math.e)
STATS = 8
PIECES = 2
PART_COST = 1000
VMEM_LIMIT = 32 * 1024 * 1024
SMALL_LIMIT = 8 * 1024 * 1024
BF16 = jnp.bfloat16
F32 = jnp.float32
VMEM = pl.BlockSpec(memory_space=pltpu.VMEM)


def power_of_two(count):
    return count & (count - 1) == 0


def peer(place, step, count):
    if power_of_two(count):
        return place ^ step
    return (place + count - step) % count


def query_rounds(inner):
    steps = list(range(1, inner))
    return [tuple(steps[n : n + 2]) for n in range(0, inner - 1, 2)]


def inner_pairs(steps, count):
    return [(2 * peer(i, steps[min(c, len(steps) - 1)], count) + c, 2 * i + c) for i in range(count) for c in range(2)]


def fetch(value, steps):
    return lax.ppermute(value, ("inner", "core"), inner_pairs(steps, lax.axis_size("inner")))


def give_back(value, steps):
    pairs = inner_pairs(steps, lax.axis_size("inner"))
    return lax.ppermute(value, ("inner", "core"), [(b, a) for a, b in pairs])


def fetch_z(value, step):
    count = lax.axis_size("z")
    return lax.ppermute(value, "z", [(peer(z, step, count), z) for z in range(count)])


def give_back_z(value, step):
    count = lax.axis_size("z")
    return lax.ppermute(value, "z", [(z, peer(z, step, count)) for z in range(count)])


def swap_cores(value):
    return lax.ppermute(value, "core", [(0, 1), (1, 0)])


def three_parts(value):
    high = value.astype(BF16).astype(F32)
    rest = value - high
    middle = rest.astype(BF16).astype(F32)
    return [high, middle, rest - middle]


def pack_rows(heads, q_ref, g_ref, o_ref, lse_ref, start_ref, pack_ref, base):
    tok = q_ref.shape[0]
    width = q_ref.shape[1] // heads
    half = tok // 2
    lanes = heads * half
    rows = []
    lse = lse_ref[...]
    starts = start_ref[...]
    for late in range(2):
        here = slice(late * half, (late + 1) * half)
        products = []
        for h in range(heads):
            cols = slice(h * width, (h + 1) * width)
            q, g = q_ref[here, cols], g_ref[here, cols]
            first = base + late * lanes + h * half
            pack_ref[first : first + half, :] = q
            pack_ref[2 * lanes + first : 2 * lanes + first + half, :] = g
            products.append(g.astype(F32) * o_ref[here, cols].astype(F32))
        delta = jnp.sum(jnp.concatenate(products, axis=0).T, axis=0, keepdims=True)
        log_part = jnp.concatenate([lse[h : h + 1, here] for h in range(heads)], axis=1)
        start = jnp.concatenate([starts[:, here]] * heads, axis=1)
        stats = three_parts(log_part) + three_parts(delta)
        stats += [(start >> 8).astype(F32), (start & 255).astype(F32)]
        for value in stats:
            rows += [value[:, c : c + width] for c in range(0, lanes, width)]
    first = base + 4 * lanes
    pack_ref[first : first + len(rows), :] = jnp.concatenate(rows, axis=0).astype(BF16)


def pack_kernel(heads, *refs):
    sources, pack_ref, places, arrived = refs[:5], refs[5], refs[6:11], refs[11]
    copies = [pltpu.make_async_copy(a, b, arrived.at[i]) for i, (a, b) in enumerate(zip(sources, places))]
    for copy in copies:
        copy.start()
    for copy in copies:
        copy.wait()
    pack_rows(heads, *places, pack_ref, 0)


def rows_packed(heads, queries):
    tok, columns = queries.shape
    return 2 * heads * tok + STATS * heads * tok // (columns // heads)


def pack(heads, args):
    args = [pltpu.with_memory_space_constraint(a, pltpu.HBM) for a in args]
    return pl.pallas_call(
        functools.partial(pack_kernel, heads),
        out_shape=jax.ShapeDtypeStruct((rows_packed(heads, args[0]), args[0].shape[1] // heads), BF16),
        in_specs=[pl.BlockSpec(memory_space=pltpu.HBM)] * 5,
        out_specs=VMEM,
        scratch_shapes=[pltpu.VMEM(a.shape, a.dtype) for a in args] + [pltpu.SemaphoreType.DMA((5,))],
        compiler_params=pltpu.CompilerParams(vmem_limit_bytes=SMALL_LIMIT),
        name="pack",
    )(*args)


def pack_chip_kernel(heads, *refs):
    own_ref, pack_ref = refs[0], refs[-1]
    rows = own_ref.shape[0]
    pack_ref[:rows, :] = own_ref[...]
    pack_rows(heads, *refs[1:6], pack_ref, rows)


def pack_chip(heads, own, args):
    return pl.pallas_call(
        functools.partial(pack_chip_kernel, heads),
        out_shape=jax.ShapeDtypeStruct((2 * own.shape[0], own.shape[1]), BF16),
        in_specs=[VMEM] * 6,
        out_specs=VMEM,
        compiler_params=pltpu.CompilerParams(vmem_limit_bytes=SMALL_LIMIT),
        name="pack_chip",
    )(own, *args)


def stack_kernel(*refs):
    out = refs[-1]
    rows = refs[0].shape[0]
    for n, ref in enumerate(refs[:-1]):
        out[n * rows : (n + 1) * rows, :] = ref[...]


def stack(*values):
    rows, columns = values[0].shape
    return pl.pallas_call(
        stack_kernel,
        out_shape=jax.ShapeDtypeStruct((len(values) * rows, columns), values[0].dtype),
        in_specs=[VMEM] * len(values),
        out_specs=VMEM,
        compiler_params=pltpu.CompilerParams(vmem_limit_bytes=SMALL_LIMIT),
        name="stack",
    )(*values)


def part_kernel(steps, first, last, heads, sizes, *refs):
    inner, zed = sizes
    pack_ref, refs = refs[0], refs[1:]
    if first:
        blocks, refs = refs[:2], refs[2:]
        dq_ref, acc_ref, k_ref, v_ref, kt_ref, dqt_ref = refs
    elif last:
        k_ref, v_ref, kt_ref, acc_in, dq_ref, kept_ref, sent_ref, dqt_ref, acc_ref = refs
    else:
        k_ref, v_ref, kt_ref, acc_in, dq_ref, acc_ref, dqt_ref = refs
    me = lax.axis_index("inner")
    z_me = lax.axis_index("z")
    core = lax.axis_index("core")
    width = dq_ref.shape[1] // heads
    tok = k_ref.shape[0] // (2 * zed)
    half = tok // 2
    lanes = heads * half
    front = zed * tok
    band_len = inner * half
    bands = 4 * zed
    scale = width**-0.5
    nt = (((1,), (1,)), ((), ()))
    per = lanes // width
    rows_each = 4 * lanes + STATS * 2 * per
    jobs = pack_ref.shape[0] // rows_each
    lane = lax.broadcasted_iota(jnp.int32, (1, lanes), 1) % half
    row = lax.broadcasted_iota(jnp.int32, (tok, 1), 0)

    if first:
        for n, block in enumerate(blocks):
            for m, s in enumerate(range(zed - 1, -1, -1)):
                source = 2 * peer(z_me, s, zed) + (1 - core if n else core)
                for late in range(2):
                    here = pl.ds(pl.multiple_of(late * front + source * half, half), half)
                    rows = slice(m * tok + late * half, m * tok + (late + 1) * half)
                    k_ref[here, :] = block[rows, :width]
                    v_ref[here, :] = block[rows, width:]
        kt_ref[...] = k_ref[...].T

    member = peer(me, jnp.where(core == 0, steps[0], steps[-1]), inner) if steps else me

    def tile(keys, values, q, g, lse, delta, mask):
        s = lax.dot_general(keys, q, nt, preferred_element_type=F32)
        dp = lax.dot_general(values, g, nt, preferred_element_type=F32)
        prob = jnp.where(mask, jnp.exp2(s * (scale * LOG2E) - lse), 0.0)
        dscore = prob * (dp - delta)
        return prob.astype(BF16), dscore.astype(BF16)

    def pick(early, pair):
        return jnp.where(early, pair[0], pair[1])

    for job in range(jobs):
        base = job * rows_each
        outer = 2 * z_me + (core if job == 0 else 1 - core)
        rows = pack_ref[base + 4 * lanes : base + rows_each, :].astype(F32)
        info = []
        for late in range(2):

            def stat(n):
                at = (late * STATS + n) * per
                return jnp.concatenate([rows[at + i : at + i + 1] for i in range(per)], axis=1)

            lse = (stat(0) + stat(1) + stat(2)) * LOG2E
            delta = stat(3) + stat(4) + stat(5)
            start = (stat(6) * 256.0 + stat(7)).astype(jnp.int32)
            band = bands - 1 - outer if late else outer
            info.append((lse, delta, start, band * band_len + member * half + lane))

        lse, delta, start, _ = info[1]
        pos = jnp.concatenate(
            [(2 * j + row // half) * band_len + me * half + row % half for j in range(zed)], axis=0
        )
        q_late = pack_ref[base + lanes : base + 2 * lanes, :]
        g_late = pack_ref[base + 3 * lanes : base + 4 * lanes, :]
        prob, dscore = tile(k_ref[:front, :], v_ref[:front, :], q_late, g_late, lse, delta, pos >= start)
        dk = jnp.dot(dscore, q_late, preferred_element_type=F32)
        dv = jnp.dot(prob, g_late, preferred_element_type=F32)
        dqt_ref[:, lanes:] = jnp.dot(kt_ref[:, :front], dscore, preferred_element_type=F32)
        dqt_ref[:, :lanes] = jnp.zeros((width, lanes), F32)
        if first:
            acc_ref[:front, :width] = dk
            acc_ref[:front, width:] = dv
            acc_ref[front:, :] = jnp.zeros((front, 2 * width), F32)
        else:
            before = acc_in if job == 0 else acc_ref
            acc_ref[:front, :width] = before[:front, :width] + dk
            acc_ref[:front, width:] = before[:front, width:] + dv
            if job == 0:
                acc_ref[front:, :] = acc_in[front:, :]

        done = []
        for t in range(zed + 1):
            early = t <= z_me
            j = jnp.where(early, t, t - 1)
            first_key = pl.multiple_of(jnp.where(early, 0, front) + j * tok, tok)
            first_query = pl.multiple_of(jnp.where(early, 0, lanes), lanes)
            source = 2 * j + row // half
            band = jnp.where(early, source, bands - 1 - source)
            pos = band * band_len + me * half + row % half
            lse, delta, start, q_pos = (pick(early, (a, b)) for a, b in zip(*info))
            keys = pl.ds(first_key, tok)
            q = pack_ref[pl.ds(pl.multiple_of(base + first_query, 16), lanes), :]
            g = pack_ref[pl.ds(pl.multiple_of(base + 2 * lanes + first_query, 16), lanes), :]
            mask = jnp.logical_and(pos <= q_pos, pos >= start)
            prob, dscore = tile(k_ref[keys, :], v_ref[keys, :], q, g, lse, delta, mask)
            done.append((keys, pl.ds(first_query, lanes), q, g, prob, dscore))
        parts = []
        for keys, here, q, g, prob, dscore in done:
            dk = jnp.dot(dscore, q, preferred_element_type=F32)
            dv = jnp.dot(prob, g, preferred_element_type=F32)
            dq = jnp.dot(kt_ref[:, keys], dscore, preferred_element_type=F32)
            parts.append((keys, here, dk, dv, dq))
        for keys, here, dk, dv, dq in parts:
            acc_ref[keys, :width] += dk
            acc_ref[keys, width:] += dv
            dqt_ref[:, here] += dq

        for late in range(2):
            turned = (dqt_ref[:, late * lanes : (late + 1) * lanes] * scale).T.astype(dq_ref.dtype)
            to = slice(job * tok + late * half, job * tok + (late + 1) * half)
            for h in range(heads):
                dq_ref[to, h * width : (h + 1) * width] = turned[h * half : (h + 1) * half]

    if last:
        low = core == 0
        for n in range(2 * zed):
            to = slice(n * half, (n + 1) * half)
            for columns, factor in ((slice(0, width), scale), (slice(width, 2 * width), 1.0)):
                one = acc_ref[n * tok : n * tok + half, columns] * factor
                two = acc_ref[n * tok + half : (n + 1) * tok, columns] * factor
                kept_ref[to, columns] = jnp.where(low, one, two)
                sent_ref[to, columns] = jnp.where(low, two, one).astype(sent_ref.dtype)


def part(steps, packed, state, last, heads, sizes, tok, width):
    zed = sizes[1]
    first = not steps
    jobs = max(1, len(steps))
    keys = 2 * zed * tok
    outs = [jax.ShapeDtypeStruct((jobs * tok, heads * width), F32 if first else BF16)]
    acc = ((keys, 2 * width), F32)
    scratch = [pltpu.VMEM((width, heads * tok), F32)]
    if last:
        outs += [jax.ShapeDtypeStruct((zed * tok, 2 * width), t) for t in (F32, BF16)]
        scratch.append(pltpu.VMEM(*acc))
    else:
        outs.append(jax.ShapeDtypeStruct(*acc))
    if first:
        outs += [jax.ShapeDtypeStruct(s, BF16) for s in ((keys, width), (keys, width), (width, keys))]
    args = [packed] + list(state)
    return pl.pallas_call(
        functools.partial(part_kernel, steps, first, last, heads, sizes),
        out_shape=outs,
        in_specs=[VMEM] * len(args),
        out_specs=[VMEM] * len(outs),
        scratch_shapes=scratch,
        compiler_params=pltpu.CompilerParams(vmem_limit_bytes=VMEM_LIMIT),
        cost_estimate=pl.CostEstimate(flops=jobs * PART_COST, bytes_accessed=1000, transcendentals=0),
        name="part",
    )(*args)


def join_kernel(zed, kept_ref, other_ref, *outs):
    z_me = lax.axis_index("z")
    tok = outs[0].shape[0]
    half = tok // 2
    for s, out in enumerate(outs):
        for late in range(2):
            here = pl.ds(pl.multiple_of((late * zed + peer(z_me, s, zed)) * half, half), half)
            both = kept_ref[here, :] + other_ref[here, :].astype(F32)
            out[late * half : (late + 1) * half, :] = both.astype(out.dtype)


def join(kept, other, zed):
    tok, two = kept.shape[0] // zed, kept.shape[1]
    outs = [jax.ShapeDtypeStruct((tok, two), F32 if s == 0 else BF16) for s in range(zed)]
    return pl.pallas_call(
        functools.partial(join_kernel, zed), out_shape=outs, in_specs=[VMEM] * 2, out_specs=[VMEM] * zed, name="join",
        compiler_params=pltpu.CompilerParams(vmem_limit_bytes=SMALL_LIMIT),
    )(kept, other)


def split_kernel(ref, *outs):
    rows = outs[0].shape[0]
    first = ref.shape[0] - rows * len(outs)
    for n, out in enumerate(outs):
        out[...] = ref[first + n * rows : first + (n + 1) * rows, :]


def split(value, pieces):
    rows, columns = value.shape
    one = jax.ShapeDtypeStruct((rows // 2 // pieces, columns), value.dtype)
    return pl.pallas_call(
        split_kernel,
        out_shape=[one] * pieces,
        in_specs=[VMEM],
        out_specs=[VMEM] * pieces,
        compiler_params=pltpu.CompilerParams(vmem_limit_bytes=SMALL_LIMIT),
        name="split",
    )(value)


def add_up(out, refs):
    rows = out.shape[0]
    whole = [ref for ref in refs if ref.shape[0] >= rows]
    pieces = [ref for ref in refs if ref.shape[0] < rows]
    step = pieces[0].shape[0] if pieces else rows
    for at in range(0, rows, step):
        value = whole[0][at : at + step, :].astype(F32)
        for ref in whole[1:]:
            value = value + ref[at : at + step, :].astype(F32)
        for n, ref in enumerate(pieces):
            if n * step % rows == at:
                value = value + ref[...].astype(F32)
        out[at : at + step, :] = value.astype(out.dtype)


def totals_kernel(counts, *refs):
    first = 0
    for count, out in zip(counts, refs[sum(counts) :]):
        add_up(out, refs[first : first + count])
        first += count


def totals(groups, rows):
    args = [value for values in groups for value in values]
    return pl.pallas_call(
        functools.partial(totals_kernel, [len(values) for values in groups]),
        out_shape=[jax.ShapeDtypeStruct((rows, values[0].shape[1]), BF16) for values in groups],
        in_specs=[VMEM] * len(args),
        out_specs=[VMEM] * len(groups),
        compiler_params=pltpu.CompilerParams(vmem_limit_bytes=SMALL_LIMIT),
        name="totals",
    )(*args)


def on_device(queries, keys_values, outputs, d_out, lse, doc_start):
    inner = lax.axis_size("inner")
    zed = lax.axis_size("z")
    heads = lse.shape[1]
    sizes = (inner, zed)
    tok, width = keys_values.shape[0], keys_values.shape[1] // 2
    rounds = query_rounds(inner)
    inputs = (queries, d_out, outputs, lse.T, doc_start.reshape(1, tok))
    own = pack(heads, inputs)
    chip = None
    if any(len(steps) == 2 for steps in rounds):
        theirs = [swap_cores(value) for value in inputs[:4]] + [swap_cores(doc_start).reshape(1, tok)]
        chip = pack_chip(heads, own, theirs)
    packs = [fetch(chip if len(steps) == 2 else own, steps) for steps in rounds]
    mine = [keys_values] + [fetch_z(keys_values, s) for s in range(1, zed)]
    far = list(range(zed - 1, -1, -1))
    arrived = stack(*[mine[s] for s in far])
    out = part((), own, [arrived, swap_cores(arrived)], False, heads, sizes, tok, width)
    dq_parts = [out[0]]
    acc, state = out[1], list(out[2:])
    returned = []
    for steps, packed in zip(rounds, packs):
        last = steps == rounds[-1]
        out = part(steps, packed, state + [acc], last, heads, sizes, tok, width)
        returned.append(give_back(out[0], steps))
        acc = out[1]
    kept, sent = out[1:]
    joined = join(kept, swap_cores(sent), zed)
    dkv_parts = [joined[0]] + [give_back_z(joined[s], s) for s in range(zed - 1, 0, -1)]
    for steps, back in zip(rounds, returned):
        dq_parts.append(back)
        if len(steps) == 2:
            back, dkv_parts[2] = lax.optimization_barrier((back, dkv_parts[2]))
            dq_parts += [swap_cores(piece) for piece in split(back, PIECES)]
    return tuple(totals([dq_parts, dkv_parts], tok))


def solution(mesh):
    inner, outer = mesh.shape["inner"], mesh.shape["outer"]
    split = Mesh(mesh.devices.reshape(inner, outer // 2, 2), ("inner", "z", "core"))
    rows = P(("inner", "z", "core"), None)
    return jax.shard_map(
        on_device,
        mesh=split,
        in_specs=(rows, rows, rows, rows, rows, P(("inner", "z", "core"))),
        out_specs=(rows, rows),
        check_vma=False,
    )
```

```python
import functools
import math

import jax
import jax.numpy as jnp
from jax import lax
from jax.experimental import pallas as pl
from jax.experimental.pallas import tpu as pltpu
from jax.sharding import Mesh
from jax.sharding import PartitionSpec as P

LOG2E = math.log2(math.e)
STATS = 8
SENDS = 2
KEY_SENDS = 2
PIECES = 2
PART_COST = 150000000
VMEM_LIMIT = 32 * 1024 * 1024
SMALL_LIMIT = 8 * 1024 * 1024
BF16 = jnp.bfloat16
F32 = jnp.float32
VMEM = pl.BlockSpec(memory_space=pltpu.VMEM)


def power_of_two(count):
    return count & (count - 1) == 0


def peer(place, step, count):
    if power_of_two(count):
        return place ^ step
    return (place + count - step) % count


def query_rounds(inner):
    steps = list(range(1, inner))
    return [tuple(steps[n : n + 2]) for n in range(0, inner - 1, 2)]


def inner_pairs(steps, count):
    return [(2 * peer(i, steps[min(c, len(steps) - 1)], count) + c, 2 * i + c) for i in range(count) for c in range(2)]


def fetch(value, steps):
    return lax.ppermute(value, ("inner", "core"), inner_pairs(steps, lax.axis_size("inner")))


def give_back(value, steps):
    pairs = inner_pairs(steps, lax.axis_size("inner"))
    return lax.ppermute(value, ("inner", "core"), [(b, a) for a, b in pairs])


def fetch_z(value, step):
    count = lax.axis_size("z")
    return lax.ppermute(value, "z", [(peer(z, step, count), z) for z in range(count)])


def give_back_z(value, step):
    count = lax.axis_size("z")
    return lax.ppermute(value, "z", [(z, peer(z, step, count)) for z in range(count)])


def swap_cores(value):
    return lax.ppermute(value, "core", [(0, 1), (1, 0)])


def three_parts(value):
    high = value.astype(BF16).astype(F32)
    rest = value - high
    middle = rest.astype(BF16).astype(F32)
    return [high, middle, rest - middle]


def pack_rows(heads, q_ref, g_ref, o_ref, lse_ref, start_ref, pack_ref, base):
    tok = q_ref.shape[0]
    width = q_ref.shape[1] // heads
    half = tok // 2
    lanes = heads * half
    rows = []
    lse = lse_ref[...]
    starts = start_ref[...]
    for late in range(2):
        here = slice(late * half, (late + 1) * half)
        products = []
        for h in range(heads):
            cols = slice(h * width, (h + 1) * width)
            q, g = q_ref[here, cols], g_ref[here, cols]
            first = base + late * lanes + h * half
            pack_ref[first : first + half, :] = q
            pack_ref[2 * lanes + first : 2 * lanes + first + half, :] = g
            products.append(g.astype(F32) * o_ref[here, cols].astype(F32))
        delta = jnp.sum(jnp.concatenate(products, axis=0).T, axis=0, keepdims=True)
        log_part = jnp.concatenate([lse[h : h + 1, here] for h in range(heads)], axis=1)
        start = jnp.concatenate([starts[:, here]] * heads, axis=1)
        stats = three_parts(log_part) + three_parts(delta)
        stats += [(start >> 8).astype(F32), (start & 255).astype(F32)]
        for value in stats:
            rows += [value[:, c : c + width] for c in range(0, lanes, width)]
    first = base + 4 * lanes
    pack_ref[first : first + len(rows), :] = jnp.concatenate(rows, axis=0).astype(BF16)


def pack_kernel(heads, *refs):
    sources, pack_ref, places, arrived = refs[:5], refs[5], refs[6:11], refs[11]
    copies = [pltpu.make_async_copy(a, b, arrived.at[i]) for i, (a, b) in enumerate(zip(sources, places))]
    for copy in copies:
        copy.start()
    for copy in copies:
        copy.wait()
    pack_rows(heads, *places, pack_ref, 0)


def rows_packed(heads, queries):
    tok, columns = queries.shape
    return 2 * heads * tok + STATS * heads * tok // (columns // heads)


def pack(heads, args):
    args = [pltpu.with_memory_space_constraint(a, pltpu.HBM) for a in args]
    return pl.pallas_call(
        functools.partial(pack_kernel, heads),
        out_shape=jax.ShapeDtypeStruct((rows_packed(heads, args[0]), args[0].shape[1] // heads), BF16),
        in_specs=[pl.BlockSpec(memory_space=pltpu.HBM)] * 5,
        out_specs=VMEM,
        scratch_shapes=[pltpu.VMEM(a.shape, a.dtype) for a in args] + [pltpu.SemaphoreType.DMA((5,))],
        compiler_params=pltpu.CompilerParams(vmem_limit_bytes=SMALL_LIMIT),
        name="pack",
    )(*args)


def pack_chip_kernel(heads, *refs):
    own_ref, pack_ref = refs[0], refs[-1]
    rows = own_ref.shape[0]
    pack_ref[:rows, :] = own_ref[...]
    pack_rows(heads, *refs[1:6], pack_ref, rows)


def pack_chip(heads, own, args):
    return pl.pallas_call(
        functools.partial(pack_chip_kernel, heads),
        out_shape=jax.ShapeDtypeStruct((2 * own.shape[0], own.shape[1]), BF16),
        in_specs=[VMEM] * 6,
        out_specs=VMEM,
        compiler_params=pltpu.CompilerParams(vmem_limit_bytes=SMALL_LIMIT),
        name="pack_chip",
    )(own, *args)


def stack_kernel(*refs):
    out = refs[-1]
    rows = refs[0].shape[0]
    for n, ref in enumerate(refs[:-1]):
        out[n * rows : (n + 1) * rows, :] = ref[...]


def stack(*values):
    rows, columns = values[0].shape
    return pl.pallas_call(
        stack_kernel,
        out_shape=jax.ShapeDtypeStruct((len(values) * rows, columns), values[0].dtype),
        in_specs=[VMEM] * len(values),
        out_specs=VMEM,
        compiler_params=pltpu.CompilerParams(vmem_limit_bytes=SMALL_LIMIT),
        name="stack",
    )(*values)


def visit_kernel(groups, side, fresh, resume, finish, heads, sizes, *refs):
    inner, zed = sizes
    refs = list(refs)

    def take(count):
        taken = refs[:count]
        del refs[:count]
        return taken

    jobs = [(g, n) for g, steps in enumerate(groups) for n in range(max(1, len(steps)))]
    packs = take(len(groups))
    if fresh:
        stack_refs = take(KEY_SENDS)
    else:
        k_ref, v_ref, kt_ref, acc_in = take(4)
    partials = take(len(jobs)) if resume else None
    dq_refs = take(len(groups) if resume else len(jobs))
    sum_refs = take(SENDS if finish and side else 1)
    if fresh:
        k_ref, v_ref, kt_ref = take(3)
    (dqt_ref,) = take(1)
    acc_ref = take(1)[0] if finish else sum_refs[0]
    me = lax.axis_index("inner")
    z_me = lax.axis_index("z")
    core = lax.axis_index("core")
    key_core = 1 - core if side else core
    keys, width = k_ref.shape
    tok = keys // zed
    half = tok // 2
    lanes = heads * half
    front = zed * half
    wide = 2 if zed % 2 == 0 else 1
    size = wide * half
    tiles = zed // wide
    band_len = inner * half
    bands = 4 * zed
    scale = width**-0.5
    nt = (((1,), (1,)), ((), ()))
    per = lanes // width
    rows_each = 4 * lanes + STATS * 2 * per
    lane = lax.broadcasted_iota(jnp.int32, (1, lanes), 1) % half

    def positions(late, chip, count):
        row = lax.broadcasted_iota(jnp.int32, (count, 1), 0)
        place = row // half
        source = 2 * jnp.where(late, chip - place, chip + place) + key_core
        return jnp.where(late, bands - 1 - source, source) * band_len + me * half + row % half

    if fresh:
        for m, s in enumerate(range(zed - 1, -1, -1)):
            chip = peer(z_me, s, zed)
            for late in range(2):
                here = pl.ds(pl.multiple_of((front + (zed - 1 - chip) * half) if late else chip * half, half), half)
                stack_ref = stack_refs[m * KEY_SENDS // zed]
                at = m % (zed // KEY_SENDS) * tok + late * half
                rows = slice(at, at + half)
                k_ref[here, :] = stack_ref[rows, :width]
                v_ref[here, :] = stack_ref[rows, width:]
        kt_ref[...] = k_ref[...].T

    def products(rows, pos, q, g, info, ordered):
        lse, delta, start, q_pos = info
        mask = pos >= start
        if ordered:
            mask = jnp.logical_and(pos <= q_pos, mask)
        s = lax.dot_general(k_ref[rows, :], q, nt, preferred_element_type=F32)
        dp = lax.dot_general(v_ref[rows, :], g, nt, preferred_element_type=F32)
        prob = jnp.where(mask, jnp.exp2(s * (scale * LOG2E) - lse), 0.0)
        dscore = (prob * (dp - delta)).astype(BF16)
        prob = prob.astype(BF16)
        return prob, dscore, q, g, rows

    def sums(prob, dscore, q, g, rows):
        return (
            jnp.dot(dscore, q, preferred_element_type=F32),
            jnp.dot(prob, g, preferred_element_type=F32),
            jnp.dot(kt_ref[:, rows], dscore, preferred_element_type=F32),
        )

    for at, (group, second) in enumerate(jobs):
        steps, pack_ref = groups[group], packs[group]
        base = second * rows_each
        outer = 2 * z_me + (1 - core if second else core)
        member = peer(me, jnp.where(core == 0, steps[0], steps[-1]), inner) if steps else me
        rows = pack_ref[base + 4 * lanes : base + rows_each, :].astype(F32)
        info = []
        for late in range(2):

            def stat(n):
                first = (late * STATS + n) * per
                return jnp.concatenate([rows[first + i : first + i + 1] for i in range(per)], axis=1)

            lse = (stat(0) + stat(1) + stat(2)) * LOG2E
            delta = stat(3) + stat(4) + stat(5)
            start = (stat(6) * 256.0 + stat(7)).astype(jnp.int32)
            band = bands - 1 - outer if late else outer
            info.append((lse, delta, start, band * band_len + member * half + lane))
        q_early, q_late, g_early, g_late = (pack_ref[base + n * lanes : base + (n + 1) * lanes, :] for n in range(4))

        early_all = slice(0, front)
        early_first = slice(0, size)
        late_first = slice(front, front + size)
        one = products(early_all, positions(False, 0, front), q_late, g_late, info[1], False)
        two = products(late_first, positions(True, zed - 1, size), q_late, g_late, info[1], True)
        three = products(early_first, positions(False, 0, size), q_early, g_early, info[0], True)
        moving = []
        for n in range(tiles - 1):
            early = n < z_me // wide
            place = jnp.where(early, n + 1, tiles - 1 - n) * size
            here = pl.ds(pl.multiple_of(jnp.where(early, 0, front) + place, size), size)
            chip = jnp.where(early, place // half, zed - 1 - place // half)
            first = base + jnp.where(early, 0, lanes)
            q = pack_ref[pl.ds(pl.multiple_of(first, 16), lanes), :]
            g = pack_ref[pl.ds(pl.multiple_of(first + 2 * lanes, 16), lanes), :]
            picked = tuple(jnp.where(early, a, b) for a, b in zip(*info))
            to = pl.ds(pl.multiple_of(jnp.where(early, 0, lanes), lanes), lanes)
            moving.append((here, to, products(here, positions(jnp.logical_not(early), chip, size), q, g, picked, True)))

        dk0, dv0, dq0 = sums(*one)
        dk1, dv1, dq1 = sums(*two)
        dk2, dv2, dq2 = sums(*three)
        moving = [(here, to, sums(*values)) for here, to, values in moving]

        dqt_ref[:, :lanes] = dq2
        dqt_ref[:, lanes:] = dq0 + dq1
        before = None if fresh and at == 0 else acc_in if not fresh and at == 0 else acc_ref
        for columns, all_early, one_early, one_late in (
            (slice(0, width), dk0, dk2, dk1),
            (slice(width, 2 * width), dv0, dv2, dv1),
        ):
            pieces = [
                (early_first, all_early[:size] + one_early),
                (slice(size, front), all_early[size:]),
                (late_first, one_late),
            ]
            for here, value in pieces:
                if here.start < here.stop:
                    acc_ref[here, columns] = value if before is None else before[here, columns] + value
        if at == 0 and front + size < keys:
            rest = slice(front + size, keys)
            acc_ref[rest, :] = jnp.zeros((keys - front - size, 2 * width), F32) if fresh else acc_in[rest, :]
        for here, to, (dk, dv, dq) in moving:
            acc_ref[here, :width] += dk
            acc_ref[here, width:] += dv
            dqt_ref[:, to] += dq

        if not resume:
            dq_refs[at][...] = dqt_ref[...]
            continue
        dq_ref = dq_refs[group]
        for late in range(2):
            part = slice(late * lanes, (late + 1) * lanes)
            turned = ((dqt_ref[:, part] + partials[at][:, part]) * scale).T.astype(dq_ref.dtype)
            to = slice(second * tok + late * half, second * tok + (late + 1) * half)
            for h in range(heads):
                dq_ref[to, h * width : (h + 1) * width] = turned[h * half : (h + 1) * half]

    if finish:
        each = sum_refs[0].shape[0]
        for n, sum_ref in enumerate(sum_refs):
            here = slice(n * each, (n + 1) * each)
            sum_ref[:, :width] = (acc_ref[here, :width] * scale).astype(sum_ref.dtype)
            sum_ref[:, width:] = acc_ref[here, width:].astype(sum_ref.dtype)


def visit(groups, side, packs, key_state, partials, finish, heads, sizes, tok, width):
    zed = sizes[1]
    fresh, resume = len(key_state) == KEY_SENDS, partials is not None
    jobs = sum(max(1, len(steps)) for steps in groups)
    keys = zed * tok
    if resume:
        outs = [
            jax.ShapeDtypeStruct((max(1, len(steps)) * tok, heads * width), BF16 if steps else F32) for steps in groups
        ]
    else:
        outs = [jax.ShapeDtypeStruct((width, heads * tok), F32)] * jobs
    count = len(outs)
    pieces = SENDS if finish and side else 1
    outs += [jax.ShapeDtypeStruct((keys // pieces, 2 * width), BF16 if finish and side else F32)] * pieces
    if fresh:
        outs += [jax.ShapeDtypeStruct(s, BF16) for s in ((keys, width), (keys, width), (width, keys))]
    scratch = [pltpu.VMEM((width, heads * tok), F32)]
    if finish:
        scratch.append(pltpu.VMEM((keys, 2 * width), F32))
    args = list(packs) + list(key_state) + list(partials or [])
    out = pl.pallas_call(
        functools.partial(visit_kernel, groups, side, fresh, resume, finish, heads, sizes),
        out_shape=outs,
        in_specs=[VMEM] * len(args),
        out_specs=[VMEM] * len(outs),
        scratch_shapes=scratch,
        compiler_params=pltpu.CompilerParams(vmem_limit_bytes=VMEM_LIMIT),
        cost_estimate=pl.CostEstimate(flops=jobs * PART_COST, bytes_accessed=1000, transcendentals=0),
        name="visit",
    )(*args)
    return out[:count], out[count : count + pieces], out[count + pieces :]


def join_kernel(zed, kept_ref, *refs):
    other_refs, outs = refs[:SENDS], refs[SENDS:]
    each = other_refs[0].shape[0]
    z_me = lax.axis_index("z")
    tok = outs[0].shape[0]
    half = tok // 2
    for s, out in enumerate(outs):
        for late in range(2):
            there = peer(z_me, s, zed)
            first = pl.multiple_of((2 * zed - 1 - there if late else there) * half, half)
            if SENDS == 2:
                other_ref, at = other_refs[late], first - late * each
            else:
                other_ref, at = other_refs[0], first
            both = kept_ref[pl.ds(first, half), :] + other_ref[pl.ds(pl.multiple_of(at, half), half), :].astype(F32)
            out[late * half : (late + 1) * half, :] = both.astype(out.dtype)


def join(kept, others, zed):
    tok, two = kept.shape[0] // zed, kept.shape[1]
    outs = [jax.ShapeDtypeStruct((tok, two), F32 if s == 0 else BF16) for s in range(zed)]
    return pl.pallas_call(
        functools.partial(join_kernel, zed), out_shape=outs, in_specs=[VMEM] * (1 + SENDS), out_specs=[VMEM] * zed, name="join",
        compiler_params=pltpu.CompilerParams(vmem_limit_bytes=SMALL_LIMIT),
    )(kept, *others)


def split_kernel(ref, *outs):
    rows = outs[0].shape[0]
    first = ref.shape[0] - rows * len(outs)
    for n, out in enumerate(outs):
        out[...] = ref[first + n * rows : first + (n + 1) * rows, :]


def split(value, pieces):
    rows, columns = value.shape
    one = jax.ShapeDtypeStruct((rows // 2 // pieces, columns), value.dtype)
    return pl.pallas_call(
        split_kernel,
        out_shape=[one] * pieces,
        in_specs=[VMEM],
        out_specs=[VMEM] * pieces,
        compiler_params=pltpu.CompilerParams(vmem_limit_bytes=SMALL_LIMIT),
        name="split",
    )(value)


def add_up(out, refs):
    rows = out.shape[0]
    whole = [ref for ref in refs if ref.shape[0] >= rows]
    pieces = [ref for ref in refs if ref.shape[0] < rows]
    step = pieces[0].shape[0] if pieces else rows
    for at in range(0, rows, step):
        value = whole[0][at : at + step, :].astype(F32)
        for ref in whole[1:]:
            value = value + ref[at : at + step, :].astype(F32)
        for n, ref in enumerate(pieces):
            if n * step % rows == at:
                value = value + ref[...].astype(F32)
        out[at : at + step, :] = value.astype(out.dtype)


def totals_kernel(counts, *refs):
    first = 0
    for count, out in zip(counts, refs[sum(counts) :]):
        add_up(out, refs[first : first + count])
        first += count


def totals(groups, rows):
    args = [value for values in groups for value in values]
    return pl.pallas_call(
        functools.partial(totals_kernel, [len(values) for values in groups]),
        out_shape=[jax.ShapeDtypeStruct((rows, values[0].shape[1]), BF16) for values in groups],
        in_specs=[VMEM] * len(args),
        out_specs=[VMEM] * len(groups),
        compiler_params=pltpu.CompilerParams(vmem_limit_bytes=SMALL_LIMIT),
        name="totals",
    )(*args)


def on_device(queries, keys_values, outputs, d_out, lse, doc_start):
    inner = lax.axis_size("inner")
    zed = lax.axis_size("z")
    heads = lse.shape[1]
    sizes = (inner, zed)
    tok, width = keys_values.shape[0], keys_values.shape[1] // 2
    rounds = query_rounds(inner)
    inputs = (queries, d_out, outputs, lse.T, doc_start.reshape(1, tok))
    own = pack(heads, inputs)
    chip = None
    if any(len(steps) == 2 for steps in rounds):
        theirs = [swap_cores(value) for value in inputs[:4]] + [swap_cores(doc_start).reshape(1, tok)]
        chip = pack_chip(heads, own, theirs)
    packs = [fetch(chip if len(steps) == 2 else own, steps) for steps in rounds]
    mine = [keys_values] + [fetch_z(keys_values, s) for s in range(1, zed)]
    far = list(range(zed - 1, -1, -1))
    each = zed // KEY_SENDS
    arrived = [stack(*[mine[s] for s in far[n * each : (n + 1) * each]]) for n in range(KEY_SENDS)]
    groups = [()] + rounds[:-1]
    firsts = [own] + packs[:-1]
    partials, mine_sums, mine_keys = visit(groups, 0, firsts, arrived, None, False, heads, sizes, tok, width)
    theirs = [swap_cores(some) for some in arrived]
    dqs, their_sums, their_keys = visit(groups, 1, firsts, theirs, partials, False, heads, sizes, tok, width)
    returned = [give_back(dq, steps) for dq, steps in zip(dqs[1:], rounds)]
    ends = rounds[-1:]
    their_state, mine_state = list(their_keys) + list(their_sums), list(mine_keys) + list(mine_sums)
    partials, sent, _ = visit(ends, 1, packs[-1:], their_state, None, True, heads, sizes, tok, width)
    (dq_last,), (kept,), _ = visit(ends, 0, packs[-1:], mine_state, partials, True, heads, sizes, tok, width)
    returned.append(give_back(dq_last, ends[0]))
    dq_parts = [dqs[0]]
    joined = join(kept, [swap_cores(some) for some in sent], zed)
    dkv_parts = [joined[0]] + [give_back_z(joined[s], s) for s in range(zed - 1, 0, -1)]
    for steps, back in zip(rounds, returned):
        dq_parts.append(back)
        if len(steps) == 2:
            back, dkv_parts[2] = lax.optimization_barrier((back, dkv_parts[2]))
            dq_parts += [swap_cores(piece) for piece in split(back, PIECES)]
    return tuple(totals([dq_parts, dkv_parts], tok))


def solution(mesh):
    inner, outer = mesh.shape["inner"], mesh.shape["outer"]
    split = Mesh(mesh.devices.reshape(inner, outer // 2, 2), ("inner", "z", "core"))
    rows = P(("inner", "z", "core"), None)
    return jax.shard_map(
        on_device,
        mesh=split,
        in_specs=(rows, rows, rows, rows, rows, P(("inner", "z", "core"))),
        out_specs=(rows, rows),
        check_vma=False,
    )
```

```python
import functools
import math

import jax
import jax.numpy as jnp
from jax import lax
from jax.experimental import pallas as pl
from jax.experimental.pallas import tpu as pltpu
from jax.sharding import Mesh
from jax.sharding import PartitionSpec as P

LOG2E = math.log2(math.e)
STATS = 8
SENDS = 2
KEY_SENDS = 2
PIECES = 2
PART_COST = 150000000
VMEM_LIMIT = 32 * 1024 * 1024
SMALL_LIMIT = 8 * 1024 * 1024
BF16 = jnp.bfloat16
F32 = jnp.float32
VMEM = pl.BlockSpec(memory_space=pltpu.VMEM)


def power_of_two(count):
    return count & (count - 1) == 0


def peer(place, step, count):
    if power_of_two(count):
        return place ^ step
    return (place + count - step) % count


def query_rounds(inner):
    steps = list(range(1, inner))
    return [tuple(steps[n : n + 2]) for n in range(0, inner - 1, 2)]


def inner_pairs(steps, count):
    return [(2 * peer(i, steps[min(c, len(steps) - 1)], count) + c, 2 * i + c) for i in range(count) for c in range(2)]


def fetch(value, steps):
    return lax.ppermute(value, ("inner", "core"), inner_pairs(steps, lax.axis_size("inner")))


def give_back(value, steps):
    pairs = inner_pairs(steps, lax.axis_size("inner"))
    return lax.ppermute(value, ("inner", "core"), [(b, a) for a, b in pairs])


def fetch_z(value, step):
    count = lax.axis_size("z")
    return lax.ppermute(value, "z", [(peer(z, step, count), z) for z in range(count)])


def give_back_z(value, step):
    count = lax.axis_size("z")
    return lax.ppermute(value, "z", [(z, peer(z, step, count)) for z in range(count)])


def swap_cores(value):
    return lax.ppermute(value, "core", [(0, 1), (1, 0)])


def three_parts(value):
    high = value.astype(BF16).astype(F32)
    rest = value - high
    middle = rest.astype(BF16).astype(F32)
    return [high, middle, rest - middle]


def pack_rows(heads, q_ref, g_ref, o_ref, lse_ref, start_ref, pack_ref, base):
    tok = q_ref.shape[0]
    width = q_ref.shape[1] // heads
    half = tok // 2
    lanes = heads * half
    rows = []
    lse = lse_ref[...]
    starts = start_ref[...]
    for late in range(2):
        here = slice(late * half, (late + 1) * half)
        products = []
        for h in range(heads):
            cols = slice(h * width, (h + 1) * width)
            q, g = q_ref[here, cols], g_ref[here, cols]
            first = base + late * lanes + h * half
            pack_ref[first : first + half, :] = q
            pack_ref[2 * lanes + first : 2 * lanes + first + half, :] = g
            products.append(g.astype(F32) * o_ref[here, cols].astype(F32))
        delta = jnp.sum(jnp.concatenate(products, axis=0).T, axis=0, keepdims=True)
        log_part = jnp.concatenate([lse[h : h + 1, here] for h in range(heads)], axis=1)
        start = jnp.concatenate([starts[:, here]] * heads, axis=1)
        stats = three_parts(log_part) + three_parts(delta)
        stats += [(start >> 8).astype(F32), (start & 255).astype(F32)]
        for value in stats:
            rows += [value[:, c : c + width] for c in range(0, lanes, width)]
    first = base + 4 * lanes
    pack_ref[first : first + len(rows), :] = jnp.concatenate(rows, axis=0).astype(BF16)


def pack_kernel(heads, *refs):
    sources, pack_ref, places, arrived = refs[:5], refs[5], refs[6:11], refs[11]
    copies = [pltpu.make_async_copy(a, b, arrived.at[i]) for i, (a, b) in enumerate(zip(sources, places))]
    for copy in copies:
        copy.start()
    for copy in copies:
        copy.wait()
    pack_rows(heads, *places, pack_ref, 0)


def rows_packed(heads, queries):
    tok, columns = queries.shape
    return 2 * heads * tok + STATS * heads * tok // (columns // heads)


def pack(heads, args):
    args = [pltpu.with_memory_space_constraint(a, pltpu.HBM) for a in args]
    return pl.pallas_call(
        functools.partial(pack_kernel, heads),
        out_shape=jax.ShapeDtypeStruct((rows_packed(heads, args[0]), args[0].shape[1] // heads), BF16),
        in_specs=[pl.BlockSpec(memory_space=pltpu.HBM)] * 5,
        out_specs=VMEM,
        scratch_shapes=[pltpu.VMEM(a.shape, a.dtype) for a in args] + [pltpu.SemaphoreType.DMA((5,))],
        compiler_params=pltpu.CompilerParams(vmem_limit_bytes=SMALL_LIMIT),
        name="pack",
    )(*args)


def pack_chip_kernel(heads, *refs):
    own_ref, pack_ref = refs[0], refs[-1]
    rows = own_ref.shape[0]
    pack_ref[:rows, :] = own_ref[...]
    pack_rows(heads, *refs[1:6], pack_ref, rows)


def pack_chip(heads, own, args):
    return pl.pallas_call(
        functools.partial(pack_chip_kernel, heads),
        out_shape=jax.ShapeDtypeStruct((2 * own.shape[0], own.shape[1]), BF16),
        in_specs=[VMEM] * 6,
        out_specs=VMEM,
        compiler_params=pltpu.CompilerParams(vmem_limit_bytes=SMALL_LIMIT),
        name="pack_chip",
    )(own, *args)


def stack_kernel(*refs):
    out = refs[-1]
    rows = refs[0].shape[0]
    for n, ref in enumerate(refs[:-1]):
        out[n * rows : (n + 1) * rows, :] = ref[...]


def stack(*values):
    rows, columns = values[0].shape
    return pl.pallas_call(
        stack_kernel,
        out_shape=jax.ShapeDtypeStruct((len(values) * rows, columns), values[0].dtype),
        in_specs=[VMEM] * len(values),
        out_specs=VMEM,
        compiler_params=pltpu.CompilerParams(vmem_limit_bytes=SMALL_LIMIT),
        name="stack",
    )(*values)


def visit_kernel(groups, side, fresh, resume, finish, heads, sizes, *refs):
    inner, zed = sizes
    refs = list(refs)

    def take(count):
        taken = refs[:count]
        del refs[:count]
        return taken

    jobs = [(g, n) for g, steps in enumerate(groups) for n in range(max(1, len(steps)))]
    packs = take(len(groups))
    if fresh:
        stack_refs = take(KEY_SENDS)
    else:
        k_ref, v_ref, kt_ref, acc_in = take(4)
    partials = take(len(jobs)) if resume else None
    dq_refs = take(len(groups) if resume else len(jobs))
    sum_refs = take(SENDS if finish and side else 1)
    if fresh:
        k_ref, v_ref, kt_ref = take(3)
    (dqt_ref,) = take(1)
    acc_ref = take(1)[0] if finish else sum_refs[0]
    me = lax.axis_index("inner")
    z_me = lax.axis_index("z")
    core = lax.axis_index("core")
    key_core = 1 - core if side else core
    keys, width = k_ref.shape
    tok = keys // zed
    half = tok // 2
    lanes = heads * half
    front = zed * half
    wide = 2 if zed % 2 == 0 else 1
    size = wide * half
    tiles = zed // wide
    band_len = inner * half
    bands = 4 * zed
    scale = width**-0.5
    nt = (((1,), (1,)), ((), ()))
    per = lanes // width
    rows_each = 4 * lanes + STATS * 2 * per
    lane = lax.broadcasted_iota(jnp.int32, (1, lanes), 1) % half

    def positions(late, chip, count):
        row = lax.broadcasted_iota(jnp.int32, (count, 1), 0)
        place = row // half
        source = 2 * jnp.where(late, chip - place, chip + place) + key_core
        return jnp.where(late, bands - 1 - source, source) * band_len + me * half + row % half

    if fresh:
        for m, s in enumerate(range(zed - 1, -1, -1)):
            chip = peer(z_me, s, zed)
            for late in range(2):
                here = pl.ds(pl.multiple_of((front + (zed - 1 - chip) * half) if late else chip * half, half), half)
                stack_ref = stack_refs[m * KEY_SENDS // zed]
                at = m % (zed // KEY_SENDS) * tok + late * half
                rows = slice(at, at + half)
                k_ref[here, :] = stack_ref[rows, :width]
                v_ref[here, :] = stack_ref[rows, width:]
        kt_ref[...] = k_ref[...].T

    def products(rows, pos, q, g, info, ordered):
        lse, delta, start, q_pos = info
        mask = pos >= start
        if ordered:
            mask = jnp.logical_and(pos <= q_pos, mask)
        s = lax.dot_general(k_ref[rows, :], q, nt, preferred_element_type=F32)
        dp = lax.dot_general(v_ref[rows, :], g, nt, preferred_element_type=F32)
        prob = jnp.where(mask, jnp.exp2(s * (scale * LOG2E) - lse), 0.0)
        dscore = (prob * (dp - delta)).astype(BF16)
        prob = prob.astype(BF16)
        return prob, dscore, q, g, rows

    def sums(prob, dscore, q, g, rows):
        return (
            jnp.dot(dscore, q, preferred_element_type=F32),
            jnp.dot(prob, g, preferred_element_type=F32),
            jnp.dot(kt_ref[:, rows], dscore, preferred_element_type=F32),
        )

    for at, (group, second) in enumerate(jobs):
        steps, pack_ref = groups[group], packs[group]
        base = second * rows_each
        outer = 2 * z_me + (1 - core if second else core)
        member = peer(me, jnp.where(core == 0, steps[0], steps[-1]), inner) if steps else me
        rows = pack_ref[base + 4 * lanes : base + rows_each, :].astype(F32)
        info = []
        for late in range(2):

            def stat(n):
                first = (late * STATS + n) * per
                return jnp.concatenate([rows[first + i : first + i + 1] for i in range(per)], axis=1)

            lse = (stat(0) + stat(1) + stat(2)) * LOG2E
            delta = stat(3) + stat(4) + stat(5)
            start = (stat(6) * 256.0 + stat(7)).astype(jnp.int32)
            band = bands - 1 - outer if late else outer
            info.append((lse, delta, start, band * band_len + member * half + lane))
        q_early, q_late, g_early, g_late = (pack_ref[base + n * lanes : base + (n + 1) * lanes, :] for n in range(4))

        early_all = slice(0, front)
        early_first = slice(0, size)
        late_first = slice(front, front + size)
        one = products(early_all, positions(False, 0, front), q_late, g_late, info[1], False)
        two = products(late_first, positions(True, zed - 1, size), q_late, g_late, info[1], True)
        three = products(early_first, positions(False, 0, size), q_early, g_early, info[0], True)
        moving = []
        for n in range(tiles - 1):
            early = n < z_me // wide
            place = jnp.where(early, n + 1, tiles - 1 - n) * size
            here = pl.ds(pl.multiple_of(jnp.where(early, 0, front) + place, size), size)
            chip = jnp.where(early, place // half, zed - 1 - place // half)
            first = base + jnp.where(early, 0, lanes)
            q = pack_ref[pl.ds(pl.multiple_of(first, 16), lanes), :]
            g = pack_ref[pl.ds(pl.multiple_of(first + 2 * lanes, 16), lanes), :]
            picked = tuple(jnp.where(early, a, b) for a, b in zip(*info))
            to = pl.ds(pl.multiple_of(jnp.where(early, 0, lanes), lanes), lanes)
            moving.append((here, to, products(here, positions(jnp.logical_not(early), chip, size), q, g, picked, True)))

        dk0, dv0, dq0 = sums(*one)
        dk1, dv1, dq1 = sums(*two)
        dk2, dv2, dq2 = sums(*three)
        moving = [(here, to, sums(*values)) for here, to, values in moving]

        dqt_ref[:, :lanes] = dq2
        dqt_ref[:, lanes:] = dq0 + dq1
        before = None if fresh and at == 0 else acc_in if not fresh and at == 0 else acc_ref
        for columns, all_early, one_early, one_late in (
            (slice(0, width), dk0, dk2, dk1),
            (slice(width, 2 * width), dv0, dv2, dv1),
        ):
            pieces = [
                (early_first, all_early[:size] + one_early),
                (slice(size, front), all_early[size:]),
                (late_first, one_late),
            ]
            for here, value in pieces:
                if here.start < here.stop:
                    acc_ref[here, columns] = value if before is None else before[here, columns] + value
        if at == 0 and front + size < keys:
            rest = slice(front + size, keys)
            acc_ref[rest, :] = jnp.zeros((keys - front - size, 2 * width), F32) if fresh else acc_in[rest, :]
        for here, to, (dk, dv, dq) in moving:
            acc_ref[here, :width] += dk
            acc_ref[here, width:] += dv
            dqt_ref[:, to] += dq

        if not resume:
            dq_refs[at][...] = dqt_ref[...]
            continue
        dq_ref = dq_refs[group]
        for late in range(2):
            part = slice(late * lanes, (late + 1) * lanes)
            turned = ((dqt_ref[:, part] + partials[at][:, part]) * scale).T.astype(dq_ref.dtype)
            to = slice(second * tok + late * half, second * tok + (late + 1) * half)
            for h in range(heads):
                dq_ref[to, h * width : (h + 1) * width] = turned[h * half : (h + 1) * half]

    if finish:
        each = sum_refs[0].shape[0]
        for n, sum_ref in enumerate(sum_refs):
            here = slice(n * each, (n + 1) * each)
            sum_ref[:, :width] = (acc_ref[here, :width] * scale).astype(sum_ref.dtype)
            sum_ref[:, width:] = acc_ref[here, width:].astype(sum_ref.dtype)


def visit(groups, side, packs, key_state, partials, finish, heads, sizes, tok, width):
    zed = sizes[1]
    fresh, resume = len(key_state) == KEY_SENDS, partials is not None
    jobs = sum(max(1, len(steps)) for steps in groups)
    keys = zed * tok
    if resume:
        outs = [
            jax.ShapeDtypeStruct((max(1, len(steps)) * tok, heads * width), BF16 if steps else F32) for steps in groups
        ]
    else:
        outs = [jax.ShapeDtypeStruct((width, heads * tok), F32)] * jobs
    count = len(outs)
    pieces = SENDS if finish and side else 1
    outs += [jax.ShapeDtypeStruct((keys // pieces, 2 * width), BF16 if finish and side else F32)] * pieces
    if fresh:
        outs += [jax.ShapeDtypeStruct(s, BF16) for s in ((keys, width), (keys, width), (width, keys))]
    scratch = [pltpu.VMEM((width, heads * tok), F32)]
    if finish:
        scratch.append(pltpu.VMEM((keys, 2 * width), F32))
    args = list(packs) + list(key_state) + list(partials or [])
    out = pl.pallas_call(
        functools.partial(visit_kernel, groups, side, fresh, resume, finish, heads, sizes),
        out_shape=outs,
        in_specs=[VMEM] * len(args),
        out_specs=[VMEM] * len(outs),
        scratch_shapes=scratch,
        compiler_params=pltpu.CompilerParams(vmem_limit_bytes=VMEM_LIMIT),
        cost_estimate=pl.CostEstimate(flops=jobs * PART_COST, bytes_accessed=1000, transcendentals=0),
        name="visit",
    )(*args)
    return out[:count], out[count : count + pieces], out[count + pieces :]


def join_kernel(zed, kept_ref, *refs):
    other_refs, outs = refs[:SENDS], refs[SENDS:]
    each = other_refs[0].shape[0]
    z_me = lax.axis_index("z")
    tok = outs[0].shape[0]
    half = tok // 2
    for s, out in enumerate(outs):
        for late in range(2):
            there = peer(z_me, s, zed)
            first = pl.multiple_of((2 * zed - 1 - there if late else there) * half, half)
            if SENDS == 2:
                other_ref, at = other_refs[late], first - late * each
            else:
                other_ref, at = other_refs[0], first
            both = kept_ref[pl.ds(first, half), :] + other_ref[pl.ds(pl.multiple_of(at, half), half), :].astype(F32)
            out[late * half : (late + 1) * half, :] = both.astype(out.dtype)


def join(kept, others, zed):
    tok, two = kept.shape[0] // zed, kept.shape[1]
    outs = [jax.ShapeDtypeStruct((tok, two), F32 if s == 0 else BF16) for s in range(zed)]
    return pl.pallas_call(
        functools.partial(join_kernel, zed), out_shape=outs, in_specs=[VMEM] * (1 + SENDS), out_specs=[VMEM] * zed, name="join",
        compiler_params=pltpu.CompilerParams(vmem_limit_bytes=SMALL_LIMIT),
    )(kept, *others)


def split_kernel(ref, *outs):
    rows = outs[0].shape[0]
    first = ref.shape[0] - rows * len(outs)
    for n, out in enumerate(outs):
        out[...] = ref[first + n * rows : first + (n + 1) * rows, :]


def split(value, pieces):
    rows, columns = value.shape
    one = jax.ShapeDtypeStruct((rows // 2 // pieces, columns), value.dtype)
    return pl.pallas_call(
        split_kernel,
        out_shape=[one] * pieces,
        in_specs=[VMEM],
        out_specs=[VMEM] * pieces,
        compiler_params=pltpu.CompilerParams(vmem_limit_bytes=SMALL_LIMIT),
        name="split",
    )(value)


def add_up(out, refs):
    rows = out.shape[0]
    whole = [ref for ref in refs if ref.shape[0] >= rows]
    pieces = [ref for ref in refs if ref.shape[0] < rows]
    step = pieces[0].shape[0] if pieces else rows
    for at in range(0, rows, step):
        value = whole[0][at : at + step, :].astype(F32)
        for ref in whole[1:]:
            value = value + ref[at : at + step, :].astype(F32)
        for n, ref in enumerate(pieces):
            if n * step % rows == at:
                value = value + ref[...].astype(F32)
        out[at : at + step, :] = value.astype(out.dtype)


def totals_kernel(counts, *refs):
    first = 0
    for count, out in zip(counts, refs[sum(counts) :]):
        add_up(out, refs[first : first + count])
        first += count


def totals(groups, rows):
    args = [value for values in groups for value in values]
    return pl.pallas_call(
        functools.partial(totals_kernel, [len(values) for values in groups]),
        out_shape=[jax.ShapeDtypeStruct((rows, values[0].shape[1]), BF16) for values in groups],
        in_specs=[VMEM] * len(args),
        out_specs=[VMEM] * len(groups),
        compiler_params=pltpu.CompilerParams(vmem_limit_bytes=SMALL_LIMIT),
        name="totals",
    )(*args)


def on_device(queries, keys_values, outputs, d_out, lse, doc_start):
    inner = lax.axis_size("inner")
    zed = lax.axis_size("z")
    heads = lse.shape[1]
    sizes = (inner, zed)
    tok, width = keys_values.shape[0], keys_values.shape[1] // 2
    rounds = query_rounds(inner)
    inputs = (queries, d_out, outputs, lse.T, doc_start.reshape(1, tok))
    own = pack(heads, inputs)
    chip = None
    if any(len(steps) == 2 for steps in rounds):
        theirs = [swap_cores(value) for value in inputs[:4]] + [swap_cores(doc_start).reshape(1, tok)]
        chip = pack_chip(heads, own, theirs)
    packs = [fetch(chip if len(steps) == 2 else own, steps) for steps in rounds]
    mine = [keys_values] + [fetch_z(keys_values, s) for s in range(1, zed)]
    far = list(range(zed - 1, -1, -1))
    each = zed // KEY_SENDS
    arrived = [stack(*[mine[s] for s in far[n * each : (n + 1) * each]]) for n in range(KEY_SENDS)]
    groups = [()] + rounds[:-1]
    firsts = [own] + packs[:-1]
    partials, mine_sums, mine_keys = visit(groups, 0, firsts, arrived, None, False, heads, sizes, tok, width)
    theirs = [swap_cores(some) for some in arrived]
    dqs, their_sums, their_keys = visit(groups, 1, firsts, theirs, partials, False, heads, sizes, tok, width)
    returned = [give_back(dq, steps) for dq, steps in zip(dqs[1:], rounds)]
    ends = rounds[-1:]
    their_state, mine_state = list(their_keys) + list(their_sums), list(mine_keys) + list(mine_sums)
    partials, sent, _ = visit(ends, 1, packs[-1:], their_state, None, True, heads, sizes, tok, width)
    (dq_last,), (kept,), _ = visit(ends, 0, packs[-1:], mine_state, partials, True, heads, sizes, tok, width)
    returned.append(give_back(dq_last, ends[0]))
    dq_parts = [dqs[0]]
    joined = join(kept, [swap_cores(some) for some in sent], zed)
    dkv_parts = [joined[0]] + [give_back_z(joined[s], s) for s in range(zed - 1, 0, -1)]
    for steps, back in zip(rounds, returned):
        dq_parts.append(back)
        if len(steps) == 2:
            last = min(2, zed - 1)
            back, dkv_parts[last] = lax.optimization_barrier((back, dkv_parts[last]))
            dq_parts += [swap_cores(piece) for piece in split(back, PIECES)]
    return tuple(totals([dq_parts, dkv_parts], tok))


def solution(mesh):
    inner, outer = mesh.shape["inner"], mesh.shape["outer"]
    split = Mesh(mesh.devices.reshape(inner, outer // 2, 2), ("inner", "z", "core"))
    rows = P(("inner", "z", "core"), None)
    return jax.shard_map(
        on_device,
        mesh=split,
        in_specs=(rows, rows, rows, rows, rows, P(("inner", "z", "core"))),
        out_specs=(rows, rows),
        check_vma=False,
    )
```

```python
import functools
import math

import jax
import jax.numpy as jnp
from jax import lax
from jax.experimental import pallas as pl
from jax.experimental.pallas import tpu as pltpu
from jax.sharding import Mesh
from jax.sharding import PartitionSpec as P

LOG2E = math.log2(math.e)
STATS = 8
SENDS = 1
KEY_SENDS = 2
PIECES = 2
PART_COST = 150000000
VMEM_LIMIT = 32 * 1024 * 1024
SMALL_LIMIT = 8 * 1024 * 1024
BF16 = jnp.bfloat16
F32 = jnp.float32
VMEM = pl.BlockSpec(memory_space=pltpu.VMEM)


def power_of_two(count):
    return count & (count - 1) == 0


def peer(place, step, count):
    if power_of_two(count):
        return place ^ step
    return (place + count - step) % count


def query_rounds(inner):
    steps = list(range(1, inner))
    return [tuple(steps[n : n + 2]) for n in range(0, inner - 1, 2)]


def inner_pairs(steps, count):
    return [(2 * peer(i, steps[min(c, len(steps) - 1)], count) + c, 2 * i + c) for i in range(count) for c in range(2)]


def fetch(value, steps):
    return lax.ppermute(value, ("inner", "core"), inner_pairs(steps, lax.axis_size("inner")))


def give_back(value, steps):
    pairs = inner_pairs(steps, lax.axis_size("inner"))
    return lax.ppermute(value, ("inner", "core"), [(b, a) for a, b in pairs])


def fetch_z(value, step):
    count = lax.axis_size("z")
    return lax.ppermute(value, "z", [(peer(z, step, count), z) for z in range(count)])


def give_back_z(value, step):
    count = lax.axis_size("z")
    return lax.ppermute(value, "z", [(z, peer(z, step, count)) for z in range(count)])


def swap_cores(value):
    return lax.ppermute(value, "core", [(0, 1), (1, 0)])


def three_parts(value):
    high = value.astype(BF16).astype(F32)
    rest = value - high
    middle = rest.astype(BF16).astype(F32)
    return [high, middle, rest - middle]


def pack_rows(heads, q_ref, g_ref, o_ref, lse_ref, start_ref, pack_ref, base):
    tok = q_ref.shape[0]
    width = q_ref.shape[1] // heads
    half = tok // 2
    lanes = heads * half
    rows = []
    lse = lse_ref[...]
    starts = start_ref[...]
    for late in range(2):
        here = slice(late * half, (late + 1) * half)
        products = []
        for h in range(heads):
            cols = slice(h * width, (h + 1) * width)
            q, g = q_ref[here, cols], g_ref[here, cols]
            first = base + late * lanes + h * half
            pack_ref[first : first + half, :] = q
            pack_ref[2 * lanes + first : 2 * lanes + first + half, :] = g
            products.append(g.astype(F32) * o_ref[here, cols].astype(F32))
        delta = jnp.sum(jnp.concatenate(products, axis=0).T, axis=0, keepdims=True)
        log_part = jnp.concatenate([lse[h : h + 1, here] for h in range(heads)], axis=1)
        start = jnp.concatenate([starts[:, here]] * heads, axis=1)
        stats = three_parts(log_part) + three_parts(delta)
        stats += [(start >> 8).astype(F32), (start & 255).astype(F32)]
        for value in stats:
            rows += [value[:, c : c + width] for c in range(0, lanes, width)]
    first = base + 4 * lanes
    pack_ref[first : first + len(rows), :] = jnp.concatenate(rows, axis=0).astype(BF16)


def pack_kernel(heads, *refs):
    sources, pack_ref, places, arrived = refs[:5], refs[5], refs[6:11], refs[11]
    copies = [pltpu.make_async_copy(a, b, arrived.at[i]) for i, (a, b) in enumerate(zip(sources, places))]
    for copy in copies:
        copy.start()
    for copy in copies:
        copy.wait()
    pack_rows(heads, *places, pack_ref, 0)


def rows_packed(heads, queries):
    tok, columns = queries.shape
    return 2 * heads * tok + STATS * heads * tok // (columns // heads)


def pack(heads, args):
    args = [pltpu.with_memory_space_constraint(a, pltpu.HBM) for a in args]
    return pl.pallas_call(
        functools.partial(pack_kernel, heads),
        out_shape=jax.ShapeDtypeStruct((rows_packed(heads, args[0]), args[0].shape[1] // heads), BF16),
        in_specs=[pl.BlockSpec(memory_space=pltpu.HBM)] * 5,
        out_specs=VMEM,
        scratch_shapes=[pltpu.VMEM(a.shape, a.dtype) for a in args] + [pltpu.SemaphoreType.DMA((5,))],
        compiler_params=pltpu.CompilerParams(vmem_limit_bytes=SMALL_LIMIT),
        name="pack",
    )(*args)


def pack_chip_kernel(heads, *refs):
    own_ref, pack_ref = refs[0], refs[-1]
    rows = own_ref.shape[0]
    pack_ref[:rows, :] = own_ref[...]
    pack_rows(heads, *refs[1:6], pack_ref, rows)


def pack_chip(heads, own, args):
    return pl.pallas_call(
        functools.partial(pack_chip_kernel, heads),
        out_shape=jax.ShapeDtypeStruct((2 * own.shape[0], own.shape[1]), BF16),
        in_specs=[VMEM] * 6,
        out_specs=VMEM,
        compiler_params=pltpu.CompilerParams(vmem_limit_bytes=SMALL_LIMIT),
        name="pack_chip",
    )(own, *args)


def stack_kernel(*refs):
    out = refs[-1]
    rows = refs[0].shape[0]
    for n, ref in enumerate(refs[:-1]):
        out[n * rows : (n + 1) * rows, :] = ref[...]


def stack(*values):
    rows, columns = values[0].shape
    return pl.pallas_call(
        stack_kernel,
        out_shape=jax.ShapeDtypeStruct((len(values) * rows, columns), values[0].dtype),
        in_specs=[VMEM] * len(values),
        out_specs=VMEM,
        compiler_params=pltpu.CompilerParams(vmem_limit_bytes=SMALL_LIMIT),
        name="stack",
    )(*values)


def visit_kernel(groups, side, fresh, resume, finish, heads, sizes, *refs):
    inner, zed = sizes
    refs = list(refs)

    def take(count):
        taken = refs[:count]
        del refs[:count]
        return taken

    jobs = [(g, n) for g, steps in enumerate(groups) for n in range(max(1, len(steps)))]
    packs = take(len(groups))
    if fresh:
        stack_refs = take(KEY_SENDS)
    else:
        k_ref, v_ref, kt_ref, acc_in = take(4)
    partials = take(len(jobs)) if resume else None
    dq_refs = take(len(groups) if resume else len(jobs))
    sum_refs = take(SENDS if finish and side else 1)
    if fresh:
        k_ref, v_ref, kt_ref = take(3)
    (dqt_ref,) = take(1)
    acc_ref = take(1)[0] if finish else sum_refs[0]
    me = lax.axis_index("inner")
    z_me = lax.axis_index("z")
    core = lax.axis_index("core")
    key_core = 1 - core if side else core
    keys, width = k_ref.shape
    tok = keys // zed
    half = tok // 2
    lanes = heads * half
    front = zed * half
    wide = 2 if zed % 2 == 0 else 1
    size = wide * half
    tiles = zed // wide
    band_len = inner * half
    bands = 4 * zed
    scale = width**-0.5
    nt = (((1,), (1,)), ((), ()))
    per = lanes // width
    rows_each = 4 * lanes + STATS * 2 * per
    lane = lax.broadcasted_iota(jnp.int32, (1, lanes), 1) % half

    def positions(late, chip, count):
        row = lax.broadcasted_iota(jnp.int32, (count, 1), 0)
        place = row // half
        source = 2 * jnp.where(late, chip - place, chip + place) + key_core
        return jnp.where(late, bands - 1 - source, source) * band_len + me * half + row % half

    if fresh:
        for m, s in enumerate(range(zed - 1, -1, -1)):
            chip = peer(z_me, s, zed)
            for late in range(2):
                here = pl.ds(pl.multiple_of((front + (zed - 1 - chip) * half) if late else chip * half, half), half)
                stack_ref = stack_refs[m * KEY_SENDS // zed]
                at = m % (zed // KEY_SENDS) * tok + late * half
                rows = slice(at, at + half)
                k_ref[here, :] = stack_ref[rows, :width]
                v_ref[here, :] = stack_ref[rows, width:]
        kt_ref[...] = k_ref[...].T

    def products(rows, pos, q, g, info, ordered):
        lse, delta, start, q_pos = info
        mask = pos >= start
        if ordered:
            mask = jnp.logical_and(pos <= q_pos, mask)
        s = lax.dot_general(k_ref[rows, :], q, nt, preferred_element_type=F32)
        dp = lax.dot_general(v_ref[rows, :], g, nt, preferred_element_type=F32)
        prob = jnp.where(mask, jnp.exp2(s * (scale * LOG2E) - lse), 0.0)
        dscore = (prob * (dp - delta)).astype(BF16)
        prob = prob.astype(BF16)
        return prob, dscore, q, g, rows

    def sums(prob, dscore, q, g, rows):
        return (
            jnp.dot(dscore, q, preferred_element_type=F32),
            jnp.dot(prob, g, preferred_element_type=F32),
            jnp.dot(kt_ref[:, rows], dscore, preferred_element_type=F32),
        )

    for at, (group, second) in enumerate(jobs):
        steps, pack_ref = groups[group], packs[group]
        base = second * rows_each
        outer = 2 * z_me + (1 - core if second else core)
        member = peer(me, jnp.where(core == 0, steps[0], steps[-1]), inner) if steps else me
        rows = pack_ref[base + 4 * lanes : base + rows_each, :].astype(F32)
        info = []
        for late in range(2):

            def stat(n):
                first = (late * STATS + n) * per
                return jnp.concatenate([rows[first + i : first + i + 1] for i in range(per)], axis=1)

            lse = (stat(0) + stat(1) + stat(2)) * LOG2E
            delta = stat(3) + stat(4) + stat(5)
            start = (stat(6) * 256.0 + stat(7)).astype(jnp.int32)
            band = bands - 1 - outer if late else outer
            info.append((lse, delta, start, band * band_len + member * half + lane))
        q_early, q_late, g_early, g_late = (pack_ref[base + n * lanes : base + (n + 1) * lanes, :] for n in range(4))

        early_all = slice(0, front)
        early_first = slice(0, size)
        late_first = slice(front, front + size)
        one = products(early_all, positions(False, 0, front), q_late, g_late, info[1], False)
        two = products(late_first, positions(True, zed - 1, size), q_late, g_late, info[1], True)
        three = products(early_first, positions(False, 0, size), q_early, g_early, info[0], True)
        moving = []
        for n in range(tiles - 1):
            early = n < z_me // wide
            place = jnp.where(early, n + 1, tiles - 1 - n) * size
            here = pl.ds(pl.multiple_of(jnp.where(early, 0, front) + place, size), size)
            chip = jnp.where(early, place // half, zed - 1 - place // half)
            first = base + jnp.where(early, 0, lanes)
            q = pack_ref[pl.ds(pl.multiple_of(first, 16), lanes), :]
            g = pack_ref[pl.ds(pl.multiple_of(first + 2 * lanes, 16), lanes), :]
            picked = tuple(jnp.where(early, a, b) for a, b in zip(*info))
            to = pl.ds(pl.multiple_of(jnp.where(early, 0, lanes), lanes), lanes)
            moving.append((here, to, products(here, positions(jnp.logical_not(early), chip, size), q, g, picked, True)))

        dk0, dv0, dq0 = sums(*one)
        dk1, dv1, dq1 = sums(*two)
        dk2, dv2, dq2 = sums(*three)
        moving = [(here, to, sums(*values)) for here, to, values in moving]

        dqt_ref[:, :lanes] = dq2
        dqt_ref[:, lanes:] = dq0 + dq1
        before = None if fresh and at == 0 else acc_in if not fresh and at == 0 else acc_ref
        for columns, all_early, one_early, one_late in (
            (slice(0, width), dk0, dk2, dk1),
            (slice(width, 2 * width), dv0, dv2, dv1),
        ):
            pieces = [
                (early_first, all_early[:size] + one_early),
                (slice(size, front), all_early[size:]),
                (late_first, one_late),
            ]
            for here, value in pieces:
                if here.start < here.stop:
                    acc_ref[here, columns] = value if before is None else before[here, columns] + value
        if at == 0 and front + size < keys:
            rest = slice(front + size, keys)
            acc_ref[rest, :] = jnp.zeros((keys - front - size, 2 * width), F32) if fresh else acc_in[rest, :]
        for here, to, (dk, dv, dq) in moving:
            acc_ref[here, :width] += dk
            acc_ref[here, width:] += dv
            dqt_ref[:, to] += dq

        if not resume:
            dq_refs[at][...] = dqt_ref[...]
            continue
        dq_ref = dq_refs[group]
        for late in range(2):
            part = slice(late * lanes, (late + 1) * lanes)
            exact = ((dqt_ref[:, part] + partials[at][:, part]) * scale).T
            turned = exact.astype(dq_ref.dtype)
            blocks = [(2 * second, turned)]
            if len(steps) == 2 and not second:
                blocks.append((1, (exact - turned.astype(F32)).astype(dq_ref.dtype)))
            for block, value in blocks:
                to = slice(block * tok + late * half, block * tok + (late + 1) * half)
                for h in range(heads):
                    dq_ref[to, h * width : (h + 1) * width] = value[h * half : (h + 1) * half]

    if finish:
        each = sum_refs[0].shape[0]
        for n, sum_ref in enumerate(sum_refs):
            here = slice(n * each, (n + 1) * each)
            sum_ref[:, :width] = (acc_ref[here, :width] * scale).astype(sum_ref.dtype)
            sum_ref[:, width:] = acc_ref[here, width:].astype(sum_ref.dtype)


def visit(groups, side, packs, key_state, partials, finish, heads, sizes, tok, width):
    zed = sizes[1]
    fresh, resume = len(key_state) == KEY_SENDS, partials is not None
    jobs = sum(max(1, len(steps)) for steps in groups)
    keys = zed * tok
    if resume:
        outs = [
            jax.ShapeDtypeStruct(((1, 1, 3)[len(steps)] * tok, heads * width), BF16 if steps else F32) for steps in groups
        ]
    else:
        outs = [jax.ShapeDtypeStruct((width, heads * tok), F32)] * jobs
    count = len(outs)
    pieces = SENDS if finish and side else 1
    outs += [jax.ShapeDtypeStruct((keys // pieces, 2 * width), BF16 if finish and side else F32)] * pieces
    if fresh:
        outs += [jax.ShapeDtypeStruct(s, BF16) for s in ((keys, width), (keys, width), (width, keys))]
    scratch = [pltpu.VMEM((width, heads * tok), F32)]
    if finish:
        scratch.append(pltpu.VMEM((keys, 2 * width), F32))
    args = list(packs) + list(key_state) + list(partials or [])
    out = pl.pallas_call(
        functools.partial(visit_kernel, groups, side, fresh, resume, finish, heads, sizes),
        out_shape=outs,
        in_specs=[VMEM] * len(args),
        out_specs=[VMEM] * len(outs),
        scratch_shapes=scratch,
        compiler_params=pltpu.CompilerParams(vmem_limit_bytes=VMEM_LIMIT),
        cost_estimate=pl.CostEstimate(flops=jobs * PART_COST, bytes_accessed=1000, transcendentals=0),
        name="visit",
    )(*args)
    return out[:count], out[count : count + pieces], out[count + pieces :]


def join_kernel(zed, kept_ref, *refs):
    other_refs, outs = refs[:SENDS], refs[SENDS:]
    each = other_refs[0].shape[0]
    z_me = lax.axis_index("z")
    tok = outs[0].shape[0]
    half = tok // 2
    for s, out in enumerate(outs):
        for late in range(2):
            there = peer(z_me, s, zed)
            first = pl.multiple_of((2 * zed - 1 - there if late else there) * half, half)
            if SENDS == 2:
                other_ref, at = other_refs[late], first - late * each
            else:
                other_ref, at = other_refs[0], first
            both = kept_ref[pl.ds(first, half), :] + other_ref[pl.ds(pl.multiple_of(at, half), half), :].astype(F32)
            out[late * half : (late + 1) * half, :] = both.astype(out.dtype)


def join(kept, others, zed):
    tok, two = kept.shape[0] // zed, kept.shape[1]
    outs = [jax.ShapeDtypeStruct((tok, two), F32 if s == 0 else BF16) for s in range(zed)]
    return pl.pallas_call(
        functools.partial(join_kernel, zed), out_shape=outs, in_specs=[VMEM] * (1 + SENDS), out_specs=[VMEM] * zed, name="join",
        compiler_params=pltpu.CompilerParams(vmem_limit_bytes=SMALL_LIMIT),
    )(kept, *others)


def split_kernel(ref, *outs):
    rows = outs[0].shape[0]
    first = ref.shape[0] - rows * len(outs)
    for n, out in enumerate(outs):
        out[...] = ref[first + n * rows : first + (n + 1) * rows, :]


def split(value, pieces):
    rows, columns = value.shape
    one = jax.ShapeDtypeStruct((rows // 3 // pieces, columns), value.dtype)
    return pl.pallas_call(
        split_kernel,
        out_shape=[one] * pieces,
        in_specs=[VMEM],
        out_specs=[VMEM] * pieces,
        compiler_params=pltpu.CompilerParams(vmem_limit_bytes=SMALL_LIMIT),
        name="split",
    )(value)


def add_up(out, refs):
    rows = out.shape[0]
    whole = [ref for ref in refs if ref.shape[0] >= rows]
    low_parts = [ref for ref in refs if ref.shape[0] == 3 * rows]
    pieces = [ref for ref in refs if ref.shape[0] < rows]
    step = pieces[0].shape[0] if pieces else rows
    for at in range(0, rows, step):
        value = whole[0][at : at + step, :].astype(F32)
        for ref in whole[1:]:
            value = value + ref[at : at + step, :].astype(F32)
        for ref in low_parts:
            value = value + ref[rows + at : rows + at + step, :].astype(F32)
        for n, ref in enumerate(pieces):
            if n * step % rows == at:
                value = value + ref[...].astype(F32)
        out[at : at + step, :] = value.astype(out.dtype)


def totals_kernel(counts, *refs):
    first = 0
    for count, out in zip(counts, refs[sum(counts) :]):
        add_up(out, refs[first : first + count])
        first += count


def totals(groups, rows):
    args = [value for values in groups for value in values]
    return pl.pallas_call(
        functools.partial(totals_kernel, [len(values) for values in groups]),
        out_shape=[jax.ShapeDtypeStruct((rows, values[0].shape[1]), BF16) for values in groups],
        in_specs=[VMEM] * len(args),
        out_specs=[VMEM] * len(groups),
        compiler_params=pltpu.CompilerParams(vmem_limit_bytes=SMALL_LIMIT),
        name="totals",
    )(*args)


def on_device(queries, keys_values, outputs, d_out, lse, doc_start):
    inner = lax.axis_size("inner")
    zed = lax.axis_size("z")
    heads = lse.shape[1]
    sizes = (inner, zed)
    tok, width = keys_values.shape[0], keys_values.shape[1] // 2
    rounds = query_rounds(inner)
    inputs = (queries, d_out, outputs, lse.T, doc_start.reshape(1, tok))
    own = pack(heads, inputs)
    chip = None
    if any(len(steps) == 2 for steps in rounds):
        theirs = [swap_cores(value) for value in inputs[:4]] + [swap_cores(doc_start).reshape(1, tok)]
        chip = pack_chip(heads, own, theirs)
    packs = [fetch(chip if len(steps) == 2 else own, steps) for steps in rounds]
    mine = [keys_values] + [fetch_z(keys_values, s) for s in range(1, zed)]
    far = list(range(zed - 1, -1, -1))
    each = zed // KEY_SENDS
    arrived = [stack(*[mine[s] for s in far[n * each : (n + 1) * each]]) for n in range(KEY_SENDS)]
    groups = [()] + rounds[:-1]
    firsts = [own] + packs[:-1]
    partials, mine_sums, mine_keys = visit(groups, 0, firsts, arrived, None, False, heads, sizes, tok, width)
    theirs = [swap_cores(some) for some in arrived]
    dqs, their_sums, their_keys = visit(groups, 1, firsts, theirs, partials, False, heads, sizes, tok, width)
    returned = [give_back(dq, steps) for dq, steps in zip(dqs[1:], rounds)]
    ends = rounds[-1:]
    their_state, mine_state = list(their_keys) + list(their_sums), list(mine_keys) + list(mine_sums)
    partials, sent, _ = visit(ends, 1, packs[-1:], their_state, None, True, heads, sizes, tok, width)
    (dq_last,), (kept,), _ = visit(ends, 0, packs[-1:], mine_state, partials, True, heads, sizes, tok, width)
    returned.append(give_back(dq_last, ends[0]))
    dq_parts = [dqs[0]]
    joined = join(kept, [swap_cores(some) for some in sent], zed)
    dkv_parts = [joined[0]] + [give_back_z(joined[s], s) for s in range(zed - 1, 0, -1)]
    for steps, back in zip(rounds, returned):
        dq_parts.append(back)
        if len(steps) == 2:
            last = min(2, zed - 1)
            back, dkv_parts[last] = lax.optimization_barrier((back, dkv_parts[last]))
            dq_parts += [swap_cores(piece) for piece in split(back, PIECES)]
    return tuple(totals([dq_parts, dkv_parts], tok))


def solution(mesh):
    inner, outer = mesh.shape["inner"], mesh.shape["outer"]
    split = Mesh(mesh.devices.reshape(inner, outer // 2, 2), ("inner", "z", "core"))
    rows = P(("inner", "z", "core"), None)
    return jax.shard_map(
        on_device,
        mesh=split,
        in_specs=(rows, rows, rows, rows, rows, P(("inner", "z", "core"))),
        out_specs=(rows, rows),
        check_vma=False,
    )
```

```python
import functools
import math

import jax
import jax.numpy as jnp
from jax import lax
from jax.experimental import pallas as pl
from jax.experimental.pallas import tpu as pltpu
from jax.sharding import Mesh
from jax.sharding import PartitionSpec as P

LOG2E = math.log2(math.e)
STATS = 8
SENDS = 1
KEY_SENDS = 2
PIECES = 2
PART_COST = 150000000
VMEM_LIMIT = 32 * 1024 * 1024
SMALL_LIMIT = 8 * 1024 * 1024
BF16 = jnp.bfloat16
F32 = jnp.float32
VMEM = pl.BlockSpec(memory_space=pltpu.VMEM)


def power_of_two(count):
    return count & (count - 1) == 0


def peer(place, step, count):
    if power_of_two(count):
        return place ^ step
    return (place + count - step) % count


def query_rounds(inner):
    steps = list(range(1, inner))
    return [tuple(steps[n : n + 2]) for n in range(0, inner - 1, 2)]


def inner_pairs(steps, count):
    return [(2 * peer(i, steps[min(c, len(steps) - 1)], count) + c, 2 * i + c) for i in range(count) for c in range(2)]


def fetch(value, steps):
    return lax.ppermute(value, ("inner", "core"), inner_pairs(steps, lax.axis_size("inner")))


def give_back(value, steps):
    pairs = inner_pairs(steps, lax.axis_size("inner"))
    return lax.ppermute(value, ("inner", "core"), [(b, a) for a, b in pairs])


def fetch_z(value, step):
    count = lax.axis_size("z")
    return lax.ppermute(value, "z", [(peer(z, step, count), z) for z in range(count)])


def give_back_z(value, step):
    count = lax.axis_size("z")
    return lax.ppermute(value, "z", [(z, peer(z, step, count)) for z in range(count)])


def swap_cores(value):
    return lax.ppermute(value, "core", [(0, 1), (1, 0)])


def three_parts(value):
    high = value.astype(BF16).astype(F32)
    rest = value - high
    middle = rest.astype(BF16).astype(F32)
    return [high, middle, rest - middle]


def pack_rows(heads, q_ref, g_ref, o_ref, lse_ref, start_ref, pack_ref, base):
    tok = q_ref.shape[0]
    width = q_ref.shape[1] // heads
    half = tok // 2
    lanes = heads * half
    rows = []
    lse = lse_ref[...]
    starts = start_ref[...]
    for late in range(2):
        here = slice(late * half, (late + 1) * half)
        products = []
        for h in range(heads):
            cols = slice(h * width, (h + 1) * width)
            q, g = q_ref[here, cols], g_ref[here, cols]
            first = base + late * lanes + h * half
            pack_ref[first : first + half, :] = q
            pack_ref[2 * lanes + first : 2 * lanes + first + half, :] = g
            products.append(g.astype(F32) * o_ref[here, cols].astype(F32))
        delta = jnp.sum(jnp.concatenate(products, axis=0).T, axis=0, keepdims=True)
        log_part = jnp.concatenate([lse[h : h + 1, here] for h in range(heads)], axis=1)
        start = jnp.concatenate([starts[:, here]] * heads, axis=1)
        stats = three_parts(log_part) + three_parts(delta)
        stats += [(start >> 8).astype(F32), (start & 255).astype(F32)]
        for value in stats:
            rows += [value[:, c : c + width] for c in range(0, lanes, width)]
    first = base + 4 * lanes
    pack_ref[first : first + len(rows), :] = jnp.concatenate(rows, axis=0).astype(BF16)


def pack_kernel(heads, *refs):
    sources, pack_ref, places, arrived = refs[:5], refs[5], refs[6:11], refs[11]
    copies = [pltpu.make_async_copy(a, b, arrived.at[i]) for i, (a, b) in enumerate(zip(sources, places))]
    for copy in copies:
        copy.start()
    for copy in copies:
        copy.wait()
    pack_rows(heads, *places, pack_ref, 0)


def rows_packed(heads, queries):
    tok, columns = queries.shape
    return 2 * heads * tok + STATS * heads * tok // (columns // heads)


def pack(heads, args):
    args = [pltpu.with_memory_space_constraint(a, pltpu.HBM) for a in args]
    return pl.pallas_call(
        functools.partial(pack_kernel, heads),
        out_shape=jax.ShapeDtypeStruct((rows_packed(heads, args[0]), args[0].shape[1] // heads), BF16),
        in_specs=[pl.BlockSpec(memory_space=pltpu.HBM)] * 5,
        out_specs=VMEM,
        scratch_shapes=[pltpu.VMEM(a.shape, a.dtype) for a in args] + [pltpu.SemaphoreType.DMA((5,))],
        compiler_params=pltpu.CompilerParams(vmem_limit_bytes=SMALL_LIMIT),
        name="pack",
    )(*args)


def pack_chip_kernel(heads, *refs):
    own_ref, pack_ref = refs[0], refs[-1]
    rows = own_ref.shape[0]
    pack_ref[:rows, :] = own_ref[...]
    pack_rows(heads, *refs[1:6], pack_ref, rows)


def pack_chip(heads, own, args):
    return pl.pallas_call(
        functools.partial(pack_chip_kernel, heads),
        out_shape=jax.ShapeDtypeStruct((2 * own.shape[0], own.shape[1]), BF16),
        in_specs=[VMEM] * 6,
        out_specs=VMEM,
        compiler_params=pltpu.CompilerParams(vmem_limit_bytes=SMALL_LIMIT),
        name="pack_chip",
    )(own, *args)


def stack_kernel(*refs):
    out = refs[-1]
    rows = refs[0].shape[0]
    for n, ref in enumerate(refs[:-1]):
        out[n * rows : (n + 1) * rows, :] = ref[...]


def stack(*values):
    rows, columns = values[0].shape
    return pl.pallas_call(
        stack_kernel,
        out_shape=jax.ShapeDtypeStruct((len(values) * rows, columns), values[0].dtype),
        in_specs=[VMEM] * len(values),
        out_specs=VMEM,
        compiler_params=pltpu.CompilerParams(vmem_limit_bytes=SMALL_LIMIT),
        name="stack",
    )(*values)


def visit_kernel(groups, side, fresh, resume, finish, heads, sizes, *refs):
    inner, zed = sizes
    refs = list(refs)

    def take(count):
        taken = refs[:count]
        del refs[:count]
        return taken

    jobs = [(g, n) for g, steps in enumerate(groups) for n in range(max(1, len(steps)))]
    packs = take(len(groups))
    if fresh:
        stack_refs = take(KEY_SENDS)
    else:
        k_ref, v_ref, kt_ref, acc_in = take(4)
    partials = take(len(jobs)) if resume else None
    dq_refs = take(len(groups) if resume else len(jobs))
    sum_refs = take(SENDS if finish and side else 1)
    if fresh:
        k_ref, v_ref, kt_ref = take(3)
    (dqt_ref,) = take(1)
    acc_ref = take(1)[0] if finish else sum_refs[0]
    me = lax.axis_index("inner")
    z_me = lax.axis_index("z")
    core = lax.axis_index("core")
    key_core = 1 - core if side else core
    keys, width = k_ref.shape
    tok = keys // zed
    half = tok // 2
    lanes = heads * half
    front = zed * half
    wide = 2 if zed % 2 == 0 else 1
    size = wide * half
    tiles = zed // wide
    band_len = inner * half
    bands = 4 * zed
    scale = width**-0.5
    nt = (((1,), (1,)), ((), ()))
    per = lanes // width
    rows_each = 4 * lanes + STATS * 2 * per
    lane = lax.broadcasted_iota(jnp.int32, (1, lanes), 1) % half

    def positions(late, chip, count):
        row = lax.broadcasted_iota(jnp.int32, (count, 1), 0)
        place = row // half
        source = 2 * jnp.where(late, chip - place, chip + place) + key_core
        return jnp.where(late, bands - 1 - source, source) * band_len + me * half + row % half

    if fresh:
        for m, s in enumerate(range(zed - 1, -1, -1)):
            chip = peer(z_me, s, zed)
            for late in range(2):
                here = pl.ds(pl.multiple_of((front + (zed - 1 - chip) * half) if late else chip * half, half), half)
                stack_ref = stack_refs[m * KEY_SENDS // zed]
                at = m % (zed // KEY_SENDS) * tok + late * half
                rows = slice(at, at + half)
                k_ref[here, :] = stack_ref[rows, :width]
                v_ref[here, :] = stack_ref[rows, width:]
        kt_ref[...] = k_ref[...].T

    def products(rows, pos, q, g, info, ordered):
        lse, delta, start, q_pos = info
        mask = pos >= start
        if ordered:
            mask = jnp.logical_and(pos <= q_pos, mask)
        s = lax.dot_general(k_ref[rows, :], q, nt, preferred_element_type=F32)
        dp = lax.dot_general(v_ref[rows, :], g, nt, preferred_element_type=F32)
        prob = jnp.where(mask, jnp.exp2(s * (scale * LOG2E) - lse), 0.0)
        dscore = (prob * (dp - delta)).astype(BF16)
        prob = prob.astype(BF16)
        return prob, dscore, q, g, rows

    def sums(prob, dscore, q, g, rows):
        return (
            jnp.dot(dscore, q, preferred_element_type=F32),
            jnp.dot(prob, g, preferred_element_type=F32),
            jnp.dot(kt_ref[:, rows], dscore, preferred_element_type=F32),
        )

    for at, (group, second) in enumerate(jobs):
        steps, pack_ref = groups[group], packs[group]
        base = second * rows_each
        outer = 2 * z_me + (1 - core if second else core)
        member = peer(me, jnp.where(core == 0, steps[0], steps[-1]), inner) if steps else me
        rows = pack_ref[base + 4 * lanes : base + rows_each, :].astype(F32)
        info = []
        for late in range(2):

            def stat(n):
                first = (late * STATS + n) * per
                return jnp.concatenate([rows[first + i : first + i + 1] for i in range(per)], axis=1)

            lse = (stat(0) + stat(1) + stat(2)) * LOG2E
            delta = stat(3) + stat(4) + stat(5)
            start = (stat(6) * 256.0 + stat(7)).astype(jnp.int32)
            band = bands - 1 - outer if late else outer
            info.append((lse, delta, start, band * band_len + member * half + lane))
        q_early, q_late, g_early, g_late = (pack_ref[base + n * lanes : base + (n + 1) * lanes, :] for n in range(4))

        early_all = slice(0, front)
        early_first = slice(0, size)
        late_first = slice(front, front + size)
        one = products(early_all, positions(False, 0, front), q_late, g_late, info[1], False)
        two = products(late_first, positions(True, zed - 1, size), q_late, g_late, info[1], True)
        three = products(early_first, positions(False, 0, size), q_early, g_early, info[0], True)
        moving = []
        for n in range(tiles - 1):
            early = n < z_me // wide
            place = jnp.where(early, n + 1, tiles - 1 - n) * size
            here = pl.ds(pl.multiple_of(jnp.where(early, 0, front) + place, size), size)
            chip = jnp.where(early, place // half, zed - 1 - place // half)
            first = base + jnp.where(early, 0, lanes)
            q = pack_ref[pl.ds(pl.multiple_of(first, 16), lanes), :]
            g = pack_ref[pl.ds(pl.multiple_of(first + 2 * lanes, 16), lanes), :]
            picked = tuple(jnp.where(early, a, b) for a, b in zip(*info))
            to = pl.ds(pl.multiple_of(jnp.where(early, 0, lanes), lanes), lanes)
            moving.append((here, to, products(here, positions(jnp.logical_not(early), chip, size), q, g, picked, True)))

        dk0, dv0, dq0 = sums(*one)
        dk1, dv1, dq1 = sums(*two)
        dk2, dv2, dq2 = sums(*three)
        moving = [(here, to, sums(*values)) for here, to, values in moving]

        dqt_ref[:, :lanes] = dq2
        dqt_ref[:, lanes:] = dq0 + dq1
        before = None if fresh and at == 0 else acc_in if not fresh and at == 0 else acc_ref
        for columns, all_early, one_early, one_late in (
            (slice(0, width), dk0, dk2, dk1),
            (slice(width, 2 * width), dv0, dv2, dv1),
        ):
            pieces = [
                (early_first, all_early[:size] + one_early),
                (slice(size, front), all_early[size:]),
                (late_first, one_late),
            ]
            for here, value in pieces:
                if here.start < here.stop:
                    acc_ref[here, columns] = value if before is None else before[here, columns] + value
        if at == 0 and front + size < keys:
            rest = slice(front + size, keys)
            acc_ref[rest, :] = jnp.zeros((keys - front - size, 2 * width), F32) if fresh else acc_in[rest, :]
        for here, to, (dk, dv, dq) in moving:
            acc_ref[here, :width] += dk
            acc_ref[here, width:] += dv
            dqt_ref[:, to] += dq

        if not resume:
            dq_refs[at][...] = dqt_ref[...]
            continue
        dq_ref = dq_refs[group]
        for late in range(2):
            part = slice(late * lanes, (late + 1) * lanes)
            exact = ((dqt_ref[:, part] + partials[at][:, part]) * scale).T
            turned = exact.astype(dq_ref.dtype)
            blocks = [(2 * second, turned)]
            if len(steps) == 2 and not second:
                blocks.append((1, (exact - turned.astype(F32)).astype(dq_ref.dtype)))
            for block, value in blocks:
                to = slice(block * tok + late * half, block * tok + (late + 1) * half)
                for h in range(heads):
                    dq_ref[to, h * width : (h + 1) * width] = value[h * half : (h + 1) * half]

    if finish:
        each = sum_refs[0].shape[0]
        for n, sum_ref in enumerate(sum_refs):
            here = slice(n * each, (n + 1) * each)
            sum_ref[:, :width] = (acc_ref[here, :width] * scale).astype(sum_ref.dtype)
            sum_ref[:, width:] = acc_ref[here, width:].astype(sum_ref.dtype)


def visit(groups, side, packs, key_state, partials, finish, heads, sizes, tok, width):
    zed = sizes[1]
    fresh, resume = len(key_state) == KEY_SENDS, partials is not None
    jobs = sum(max(1, len(steps)) for steps in groups)
    keys = zed * tok
    if resume:
        outs = [
            jax.ShapeDtypeStruct(((1, 1, 3)[len(steps)] * tok, heads * width), BF16 if steps else F32) for steps in groups
        ]
    else:
        outs = [jax.ShapeDtypeStruct((width, heads * tok), F32)] * jobs
    count = len(outs)
    pieces = SENDS if finish and side else 1
    outs += [jax.ShapeDtypeStruct((keys // pieces, 2 * width), BF16 if finish and side else F32)] * pieces
    if fresh:
        outs += [jax.ShapeDtypeStruct(s, BF16) for s in ((keys, width), (keys, width), (width, keys))]
    scratch = [pltpu.VMEM((width, heads * tok), F32)]
    if finish:
        scratch.append(pltpu.VMEM((keys, 2 * width), F32))
    args = list(packs) + list(key_state) + list(partials or [])
    out = pl.pallas_call(
        functools.partial(visit_kernel, groups, side, fresh, resume, finish, heads, sizes),
        out_shape=outs,
        in_specs=[VMEM] * len(args),
        out_specs=[VMEM] * len(outs),
        scratch_shapes=scratch,
        compiler_params=pltpu.CompilerParams(vmem_limit_bytes=VMEM_LIMIT),
        cost_estimate=pl.CostEstimate(flops=jobs * PART_COST, bytes_accessed=1000, transcendentals=0),
        name="visit",
    )(*args)
    return out[:count], out[count : count + pieces], out[count + pieces :]


def join_kernel(zed, kept_ref, *refs):
    other_refs, outs = refs[:SENDS], refs[SENDS:]
    each = other_refs[0].shape[0]
    z_me = lax.axis_index("z")
    tok = outs[0].shape[0]
    half = tok // 2
    for s, out in enumerate(outs):
        for late in range(2):
            there = peer(z_me, s, zed)
            first = pl.multiple_of((2 * zed - 1 - there if late else there) * half, half)
            if SENDS == 2:
                other_ref, at = other_refs[late], first - late * each
            else:
                other_ref, at = other_refs[0], first
            both = kept_ref[pl.ds(first, half), :] + other_ref[pl.ds(pl.multiple_of(at, half), half), :].astype(F32)
            out[late * half : (late + 1) * half, :] = both.astype(out.dtype)


def join(kept, others, zed):
    tok, two = kept.shape[0] // zed, kept.shape[1]
    outs = [jax.ShapeDtypeStruct((tok, two), F32 if s == 0 else BF16) for s in range(zed)]
    return pl.pallas_call(
        functools.partial(join_kernel, zed), out_shape=outs, in_specs=[VMEM] * (1 + SENDS), out_specs=[VMEM] * zed, name="join",
        compiler_params=pltpu.CompilerParams(vmem_limit_bytes=SMALL_LIMIT),
    )(kept, *others)


def split_kernel(ref, *outs):
    rows = outs[0].shape[0]
    first = ref.shape[0] - rows * len(outs)
    for n, out in enumerate(outs):
        out[...] = ref[first + n * rows : first + (n + 1) * rows, :]


def split(value, pieces):
    rows, columns = value.shape
    one = jax.ShapeDtypeStruct((rows // 3 // pieces, columns), value.dtype)
    return pl.pallas_call(
        split_kernel,
        out_shape=[one] * pieces,
        in_specs=[VMEM],
        out_specs=[VMEM] * pieces,
        compiler_params=pltpu.CompilerParams(vmem_limit_bytes=SMALL_LIMIT),
        name="split",
    )(value)


def add_up(out, refs):
    rows = out.shape[0]
    whole = [ref for ref in refs if ref.shape[0] >= rows]
    low_parts = [ref for ref in refs if ref.shape[0] == 3 * rows]
    pieces = [ref for ref in refs if ref.shape[0] < rows]
    step = pieces[0].shape[0] if pieces else rows
    for at in range(0, rows, step):
        value = whole[0][at : at + step, :].astype(F32)
        for ref in whole[1:]:
            value = value + ref[at : at + step, :].astype(F32)
        for ref in low_parts:
            value = value + ref[rows + at : rows + at + step, :].astype(F32)
        for n, ref in enumerate(pieces):
            if n * step % rows == at:
                value = value + ref[...].astype(F32)
        out[at : at + step, :] = value.astype(out.dtype)


def totals_kernel(counts, *refs):
    first = 0
    for count, out in zip(counts, refs[sum(counts) :]):
        add_up(out, refs[first : first + count])
        first += count


def totals(groups, rows):
    args = [value for values in groups for value in values]
    return pl.pallas_call(
        functools.partial(totals_kernel, [len(values) for values in groups]),
        out_shape=[jax.ShapeDtypeStruct((rows, values[0].shape[1]), BF16) for values in groups],
        in_specs=[VMEM] * len(args),
        out_specs=[VMEM] * len(groups),
        compiler_params=pltpu.CompilerParams(vmem_limit_bytes=SMALL_LIMIT),
        name="totals",
    )(*args)


def on_device(queries, keys_values, outputs, d_out, lse, doc_start):
    inner = lax.axis_size("inner")
    zed = lax.axis_size("z")
    heads = lse.shape[1]
    sizes = (inner, zed)
    tok, width = keys_values.shape[0], keys_values.shape[1] // 2
    rounds = query_rounds(inner)
    inputs = (queries, d_out, outputs, lse.T, doc_start.reshape(1, tok))
    own = pack(heads, inputs)
    chip = None
    if any(len(steps) == 2 for steps in rounds):
        theirs = [swap_cores(value) for value in inputs[:4]] + [swap_cores(doc_start).reshape(1, tok)]
        chip = pack_chip(heads, own, theirs)
    packs = [fetch(chip if len(steps) == 2 else own, steps) for steps in rounds]
    mine = [keys_values] + [fetch_z(keys_values, s) for s in range(1, zed)]
    far = list(range(zed - 1, -1, -1))
    each = zed // KEY_SENDS
    arrived = [stack(*[mine[s] for s in far[n * each : (n + 1) * each]]) for n in range(KEY_SENDS)]
    groups = [()] + rounds[:-1]
    firsts = [own] + packs[:-1]
    partials, mine_sums, mine_keys = visit(groups, 0, firsts, arrived, None, False, heads, sizes, tok, width)
    theirs = [swap_cores(some) for some in arrived]
    dqs, their_sums, their_keys = visit(groups, 1, firsts, theirs, partials, False, heads, sizes, tok, width)
    returned = [give_back(dq, steps) for dq, steps in zip(dqs[1:], rounds)]
    ends = rounds[-1:]
    their_state, mine_state = list(their_keys) + list(their_sums), list(mine_keys) + list(mine_sums)
    partials, sent, _ = visit(ends, 1, packs[-1:], their_state, None, True, heads, sizes, tok, width)
    (dq_last,), (kept,), _ = visit(ends, 0, packs[-1:], mine_state, partials, True, heads, sizes, tok, width)
    returned.append(give_back(dq_last, ends[0]))
    dq_parts = [dqs[0]]
    joined = join(kept, [swap_cores(some) for some in sent], zed)
    dkv_parts = [joined[0]] + [give_back_z(joined[s], s) for s in range(zed - 1, 0, -1)]
    for steps, back in zip(rounds, returned):
        dq_parts.append(back)
        if len(steps) == 2:
            last = min(1, zed - 1)
            back, dkv_parts[last] = lax.optimization_barrier((back, dkv_parts[last]))
            dq_parts += [swap_cores(piece) for piece in split(back, PIECES)]
    return tuple(totals([dq_parts, dkv_parts], tok))


def solution(mesh):
    inner, outer = mesh.shape["inner"], mesh.shape["outer"]
    split = Mesh(mesh.devices.reshape(inner, outer // 2, 2), ("inner", "z", "core"))
    rows = P(("inner", "z", "core"), None)
    return jax.shard_map(
        on_device,
        mesh=split,
        in_specs=(rows, rows, rows, rows, rows, P(("inner", "z", "core"))),
        out_specs=(rows, rows),
        check_vma=False,
    )
```
